256 devices in a mesh: tile: 32 (over y, z), grp: 8 (over x, core).
Axes of the slice: x: 4, y: 4, z: 8, core: 2. Of those that a mesh axis runs over, the one named last changes fastest.
Arguments:
- state: bfloat16 [512, 1024, 556], P('tile', 'grp'), may hold values from -6 to 6
- courant: bfloat16 [512, 1024, 2], P('tile', 'grp'), may hold values from -0.44921875 to 0.44921875
- route: int32 [32, 8, 2048, 1], P('tile', 'grp'), may hold values from 0 to 31; in each aligned block of 2048 rows (0 to 2047, 2048 to 4095, ..., all dimensions but the last counted through in order) at most 96 rows name the same one
- counts: int32 [512], P('tile'), may hold values from 128 to 1024, as said below
- w_in: bfloat16 [32, 556, 512], P('tile'), may hold values from -0.25 to 0.25
- w_mid: bfloat16 [32, 3, 512, 512], P('tile'), may hold values from -0.375 to 0.375
- w_out: bfloat16 [32, 512, 368], P('tile'), may hold values from -0.375 to 0.375
Outputs:
- advected: bfloat16 [512, 1024, 556], P('tile', 'grp')
- tendency: bfloat16 [512, 1024, 368], P('tile', 'grp')
The draws below stay inside these ranges and needn't reach their ends.
Inputs may be any that keep to these rules, and one draw needn't show every extreme that they name: `route`: each column names one expert; at most 96 columns of one device name the same expert, and some expert reaches it. `counts`: rows of the middle half of latitudes are full.
All inputs are finite; a program needn't handle non-finite values.
Results may differ from the reference program's by a relative error of at most 0.008.
Values may be sent and summed in bfloat16 or wider, within the bound.
A program may use at most 128 MiB of HBM per device.

```python
import math
import jax
import jax.numpy as jnp
import numpy as np
from jax import lax

F = 556
HID = 512
OUTW = 368
NMID = 3
STEPS = 2
LAT_DEV = 16
LON_DEV = 128
COLS_DEV = 2048
NLAT = 512
NLON = 1024
MEMBERS = 32
CAP = 96
N_TILE = 32
N_GRP = 8


def draw_counts(key, part):
    key = jax.random.fold_in(key, 11)
    base = jax.random.randint(key, (NLAT,), max(1, NLON // 8), NLON + 1)
    rows = jnp.arange(NLAT)
    middle = (rows >= NLAT // 4) & (rows < NLAT - NLAT // 4)
    return jnp.where(middle, NLON, base).astype(jnp.int32)


def block_levels(stream_key, extent, pieces, low, high):
    def one(dim, parts):
        heights = jax.random.uniform(jax.random.fold_in(jax.random.fold_in(stream_key, 6), dim), (parts,), jnp.float32, low / len(pieces), high / len(pieces))
        return jnp.repeat(jnp.exp(heights), extent[dim] // parts).reshape((-1,) + (1,) * (len(extent) - dim - 1))

    factor_of = one(*pieces[0])
    for cut in pieces[1:]:
        factor_of = factor_of * one(*cut)
    return factor_of


def routed_block(own_key, own, number, rows, count, top, limit, slope):
    order = jax.random.permutation(own_key, count)
    crowded, usual = load_shares(count, rows * top, limit, slope, True), load_shares(count, rows * top, limit, slope, False)
    places = jnp.arange(count)

    def named(lengths, rotation):
        used = int((lengths > 0).sum())
        fixed = max(1, used // 4)
        moved = fixed + (places - fixed + rotation * (used - fixed)) % max(1, count - fixed)
        return jnp.zeros((count,), jnp.int32).at[order[jnp.where(places < fixed, places, moved)]].set(jnp.asarray(lengths, jnp.int32))

    lengths = jnp.where(number % 4 == 0, named(crowded, number // 4), named(usual, number - number // 4 - 1))
    mixed = jax.random.permutation(jax.random.fold_in(own, 3), count)
    source_of, receiver = mixed[0:count // 2 * 2:2], mixed[1:count // 2 * 2:2]
    room = jnp.minimum(lengths[source_of] - 1, limit - lengths[receiver]) // 2
    room = jnp.where((source_of == order[0]) | (receiver == order[0]) | (lengths[receiver] == 0), 0, jnp.maximum(room, 0))
    moved = jax.random.randint(jax.random.fold_in(own, 4), (count // 2,), 0, 1 << 20) % (room + 1)
    lengths = lengths.at[source_of].add(-moved).at[receiver].add(moved)
    items = jnp.searchsorted(jnp.cumsum(lengths), jnp.arange(rows * top), side="right").astype(jnp.int32)
    table = items.reshape(top, rows).T
    table = table[jax.random.permutation(jax.random.fold_in(own, 1), rows)]
    rotation = jax.random.randint(jax.random.fold_in(own, 2), (rows, 1), 0, top)
    return jnp.take_along_axis(table, (jnp.arange(top)[None, :] + rotation) % top, axis=1)


def load_shares(count, total, reach, slope, full):
    loads = [(1 << 20) // math.isqrt(standing ** slope) + 1 for standing in range(1, count + 1)]
    largest = reach if full else min(reach, max(-(-total // count), total * loads[0] // sum(loads)))
    least = 1 if total - largest >= count - 1 else 0
    given, rest = [largest] + [least] * (count - 1), total - largest - least * (count - 1)
    while rest > 0:
        candidates = [i for i in range(1, count) if given[i] < largest] or [i for i in range(1, count) if given[i] < reach]
        whole, left = sum([loads[i] for i in candidates]), rest
        for i in candidates:
            addition = min(reach - given[i], max(1, left * loads[i] // whole), rest)
            given[i] = given[i] + addition
            rest = rest - addition
    return np.array(given)


def noise(key, extent, deviation, most, cuts=(), held_as=jnp.bfloat16):
    drawn = jax.random.normal(key, extent, jnp.float32) * deviation
    if len(cuts) > 0:
        drawn = block_levels(key, extent, cuts, -0.22, 0.18) * drawn
    return jnp.clip(drawn, min=-most, max=most).astype(held_as)


def setup_inputs(seed: int = 0) -> dict:
    seeds = jax.random.split(jax.random.key(seed), 8)
    state = noise(seeds[0], (NLAT, NLON, F), 1.0, 6.0, ((0, 32), (1, 8)))
    courant = jnp.clip(jax.random.uniform(seeds[1], (NLAT, NLON, 2), jnp.float32, -0.44921875, 0.44921875) * block_levels(seeds[1], (NLAT, NLON, 2), ((0, 32), (1, 8)), -0.4, 0.0), -0.44921875, 0.44921875).astype(jnp.bfloat16)
    route_keys = jax.random.split(jax.random.fold_in(seeds[2], 1), N_TILE * N_GRP * COLS_DEV // COLS_DEV)
    route_turns = jax.random.permutation(jax.random.fold_in(seeds[2], 3), N_TILE * N_GRP * COLS_DEV // COLS_DEV)
    route = jax.vmap(lambda own, number: routed_block(jax.random.fold_in(seeds[2], 2), own, number, COLS_DEV, N_TILE, 1, CAP, 2))(route_keys, route_turns).reshape((N_TILE, N_GRP, COLS_DEV, 1))
    counts = draw_counts(jax.random.fold_in(seeds[7], 71), 0)
    w_in = noise(seeds[4], (MEMBERS, F, HID), F ** -0.5, 0.25, ((0, 32),))
    w_mid = noise(seeds[5], (MEMBERS, NMID, HID, HID), (HID // 2) ** -0.5, 0.375, ((0, 32),))
    w_out = noise(seeds[6], (MEMBERS, HID, OUTW), (HID // 2) ** -0.5, 0.375, ((0, 32),))
    return dict(state=state, courant=courant, route=route, counts=counts, w_in=w_in, w_mid=w_mid, w_out=w_out)


def substep(q, cour):
    padded = jnp.pad(q, ((1, 1), (0, 0), (0, 0)))
    north = padded[2:]
    south = padded[:-2]
    east = jnp.roll(q, -1, axis=1)
    west = jnp.roll(q, 1, axis=1)
    u = cour[:, :, 0:1]
    v = cour[:, :, 1:2]
    return q - (jnp.maximum(u, 0.0) * (q - west) + jnp.minimum(u, 0.0) * (east - q)) - (jnp.maximum(v, 0.0) * (q - south) + jnp.minimum(v, 0.0) * (north - q))


def apply_net(rows, first, middle, last):
    hidden = jax.nn.leaky_relu(jnp.dot(rows, first, preferred_element_type=jnp.float32), 0.15).astype(jnp.bfloat16)
    for layer in range(NMID):
        hidden = jax.nn.leaky_relu(jnp.dot(hidden, middle[layer], preferred_element_type=jnp.float32), 0.15).astype(jnp.bfloat16)
    return jnp.dot(hidden, last, preferred_element_type=jnp.float32).astype(jnp.bfloat16)


def to_blocks(grid):
    width = grid.shape[-1]
    blocks = grid.reshape(N_TILE, LAT_DEV, N_GRP, LON_DEV, width).transpose(0, 2, 1, 3, 4)
    return blocks.reshape(N_TILE * N_GRP * COLS_DEV, width)


def reference(state, courant, route, counts, w_in, w_mid, w_out):
    cour = courant.astype(jnp.float32)
    q = state.astype(jnp.float32)
    for step in range(STEPS):
        rounded = lax.optimization_barrier(substep(q, cour).astype(jnp.bfloat16))
        q = rounded.astype(jnp.float32)
    advected = rounded
    lon_index = jnp.arange(NLON, dtype=jnp.int32)
    active = (lon_index[None, :] < counts[:, None]).astype(jnp.int32)
    active_cols = to_blocks(active[:, :, None])[:, 0] > 0
    cols = to_blocks(advected)
    x = jnp.where(active_cols[:, None], cols, jnp.zeros_like(cols))
    sources = N_TILE * N_GRP
    member = route.reshape(sources, COLS_DEV)
    onehot = (member[:, :, None] == jnp.arange(N_TILE, dtype=jnp.int32)[None, None, :]).astype(jnp.int32)
    slot = jnp.sum((jnp.cumsum(onehot, axis=1) - 1) * onehot, axis=2)
    place = (jnp.arange(sources, dtype=jnp.int32)[:, None] * CAP + slot).reshape(-1)
    member = member.reshape(-1)
    buffer = jnp.zeros((N_TILE, sources * CAP, F), jnp.bfloat16).at[member, place].set(x)
    results = lax.map(lambda args: apply_net(*args), (buffer, w_in, w_mid, w_out))
    tend = results[member, place]
    tend = jnp.where(active_cols[:, None], tend, jnp.zeros_like(tend))
    tend = tend.reshape(N_TILE, N_GRP, LAT_DEV, LON_DEV, OUTW).transpose(0, 2, 1, 3, 4).reshape(NLAT, NLON, OUTW)
    return advected, tend
```

```python
import jax
import jax.numpy as jnp
from jax import lax
from jax.experimental import pallas as pl
from jax.experimental.pallas import tpu as pltpu
from jax.sharding import PartitionSpec as P

BF = jnp.bfloat16
F32 = jnp.float32
MESH = pl.DeviceIdType.MESH

F, HID, OUTW, NMID = 556, 512, 368, 3
LAT, LON, COLS = 16, 128, 2048
CAP = 96
NEXP = 32
NTILE = 32
MAIN = 512
KIN = 576
ROWS_OUT = 4 * CAP + CAP // 2
ROWS_RET = 3 * CAP
W_MID = 4 * KIN
W_OUT = W_MID + NMID * 4 * HID
W_ROWS = W_OUT + 3 * HID
CHUNKS = 24
CH = W_ROWS // CHUNKS
LAG = 2
GB = 4
NG = NEXP // GB
LANES = [(0, 128), (128, 256), (256, 384), (384, 512), (512, F)]
ADV_POINTS = 7
POINTS = CHUNKS + 3 * LAG


def kernel(
    counts_ref, route_ref, state_hbm, cour_hbm, win_hbm, wmid_hbm, wout_hbm,
    adv_hbm, tend_ref,
    q0, q1, adv, xt, cour, ub, vb, nsh, ews, ewr, ewfs, ewfr, place, pcol, pmat,
    send, recv, rs, rr, wts, wi, wm, wo, xin,
    lsem, hs_sem, hr_sem, w_s1, w_s2, w_r, f_s, f_r, r_s, r_r,
):
    t = lax.axis_index("tile")
    g = lax.axis_index("grp")
    y, z, x, c = t // 8, t % 8, g // 2, g % 2

    def dest(k):
        j = lax.rem(k * 13, NEXP)
        return lax.rem(y + j // 8, 4), lax.rem(x + (j // 2) % 4, 4), lax.rem(c + j % 2, 2)

    def dest_id(k):
        ty, tx, tc = dest(k)
        return {"tile": ty * 8 + z, "grp": tx * 2 + tc}

    def dest_base(k):
        ty, tx, tc = dest(k)
        return (ty * 8 + tx + 4 * tc) * CAP

    def source_id(k):
        j = lax.rem(k * 13, NEXP)
        ty = lax.rem(y + 4 - j // 8, 4)
        tx = lax.rem(x + 4 - (j // 2) % 4, 4)
        return {"tile": ty * 8 + z, "grp": tx * 2 + lax.rem(c + j % 2, 2)}

    def ring_id(d):
        return {"tile": y * 8 + lax.rem(z + d + 8, 8)}

    def tile_id(d):
        return {"tile": lax.rem(t + d + NTILE, NTILE)}

    def grp_id(d):
        return {"grp": lax.rem(g + d + 8, 8)}

    rel = lax.rem(z + 8 - (x + 4 * c), 8)
    forward_up = (rel >= 1) & (rel <= 3)
    forward_down = rel >= 6
    hop = jnp.where(rel <= 4, rel, 8 - rel)

    cp_state = pltpu.make_async_copy(state_hbm, q0, lsem.at[0])
    cp_cour = pltpu.make_async_copy(cour_hbm, cour, lsem.at[1])
    cp_wi = pltpu.make_async_copy(win_hbm, wi, lsem.at[2])
    cp_wm = pltpu.make_async_copy(wmid_hbm, wm, lsem.at[3])
    cp_wo = pltpu.make_async_copy(wout_hbm, wo, lsem.at[4])
    cp_adv = pltpu.make_async_copy(adv, adv_hbm, lsem.at[5])
    cp_state.start()
    cp_cour.start()

    @pl.when(rel == 0)
    def _():
        cp_wi.start()
        cp_wm.start()
        cp_wo.start()

    barrier = pltpu.get_barrier_semaphore()

    def greet(k, carry):
        pl.semaphore_signal(barrier, inc=1, device_id=dest_id(k), device_id_type=MESH)
        return carry

    lax.fori_loop(1, NEXP, greet, 0)
    for d in (1, -1):
        pl.semaphore_signal(barrier, inc=1, device_id=ring_id(d), device_id_type=MESH)
        pl.semaphore_signal(barrier, inc=1, device_id=tile_id(d), device_id_type=MESH)
        pl.semaphore_signal(barrier, inc=1, device_id=grp_id(d), device_id_type=MESH)

    def halo(n, src, dst, device):
        return pltpu.make_async_remote_copy(
            src, dst, hs_sem.at[n], hr_sem.at[n], device_id=device, device_id_type=MESH
        )

    def halos(step, q):
        b = 4 * step
        return [
            halo(b, q.at[0], nsh.at[2 * step], tile_id(-1)),
            halo(b + 1, q.at[LAT - 1], nsh.at[2 * step + 1], tile_id(1)),
            halo(b + 2, ews.at[2 * step], ewr.at[2 * step], grp_id(-1)),
            halo(b + 3, ews.at[2 * step + 1], ewr.at[2 * step + 1], grp_id(1)),
        ]

    halo0, halo1 = halos(0, q0), halos(1, q1)

    def wcopy(k, d, sem):
        part = wts.at[pl.ds(pl.multiple_of(k * CH, CH), CH)]
        return pltpu.make_async_remote_copy(
            part, part, sem.at[k], w_r.at[k], device_id=ring_id(d), device_id_type=MESH
        )

    def ring_point(p):
        k = p - LAG * hop
        ok = (k >= 0) & (k < CHUNKS)

        @pl.when(ok & (rel == 0))
        def _():
            wcopy(k, 1, w_s1).start()
            wcopy(k, -1, w_s2).start()

        @pl.when(ok & forward_up)
        def _():
            wcopy(k, 1, w_s1).wait_recv()
            wcopy(k, 1, w_s1).start()

        @pl.when(ok & forward_down)
        def _():
            wcopy(k, -1, w_s1).wait_recv()
            wcopy(k, -1, w_s1).start()

    def ring_points(a, b):
        def one(p, carry):
            ring_point(p)
            return carry

        lax.fori_loop(a, b, one, 0)

    edge_no = lax.broadcasted_iota(jnp.int32, (LAT, 128), 0)

    def put_edge(n, i, a, b, row):
        ewfs[n, :, a:b] = jnp.where(edge_no[:, : b - a] == i, row, ewfs[n, :, a:b])

    def edges_of(i, carry):
        for a, b in LANES:
            put_edge(0, i, a, b, q0[i, 0:16, a:b].astype(F32)[0:1])
            put_edge(1, i, a, b, q0[i, LON - 16 : LON, a:b].astype(F32)[15:16])
        return carry

    cp_state.wait()
    lax.fori_loop(0, LAT, edges_of, 0)
    ews[0] = ewfs[0].astype(BF)
    ews[1] = ewfs[1].astype(BF)

    @pl.when(rel == 0)
    def _():
        cp_wi.wait()
        cp_wm.wait()
        cp_wo.wait()
        for n in range(4):
            wts[n * KIN + 544 : (n + 1) * KIN, :] = jnp.zeros((KIN - 544, 128), BF)
            wts[n * KIN : n * KIN + F, :] = wi[0, :, n * 128 : (n + 1) * 128]
        for k in range(NMID):
            for n in range(4):
                r = W_MID + (k * 4 + n) * HID
                wts[r : r + HID, :] = wm[0, k, :, n * 128 : (n + 1) * 128]
        for n in range(2):
            r = W_OUT + n * HID
            wts[r : r + HID, :] = wo[0, :, n * 128 : (n + 1) * 128]
        r = W_OUT + 2 * HID
        wts[r : r + HID, :] = jnp.zeros((HID, 128), BF)
        wts[r : r + HID, 0 : OUTW - 256] = wo[0, :, 256:OUTW]

    pl.semaphore_wait(barrier, NEXP - 1 + 6)
    for h in (halo0[2], halo0[3], halo0[0], halo0[1]):
        h.start()

    cp_cour.wait()

    def spread(i, carry):
        both = cour[i].astype(F32)
        ub[i] = jnp.broadcast_to(both[:, 0:1], (LON, 128))
        vb[i] = jnp.broadcast_to(both[:, 1:2], (LON, 128))
        return carry

    lax.fori_loop(0, LAT, spread, 0)

    lat_no = lax.broadcasted_iota(jnp.int32, (LAT, LON), 0)
    lon_no = lax.broadcasted_iota(jnp.int32, (LAT, LON), 1) + g * LON
    reach = jnp.zeros((LAT, LON), jnp.int32)
    for i in range(LAT):
        reach = jnp.where(lat_no == i, counts_ref[i], reach)
    member = jnp.where(lon_no < reach, route_ref[...], -1)
    named = jnp.concatenate([(member == m).astype(F32) for m in range(NEXP)], axis=0).astype(BF)
    before = (
        lax.broadcasted_iota(jnp.int32, (LON, LON), 0)
        < lax.broadcasted_iota(jnp.int32, (LON, LON), 1)
    )
    within = jnp.dot(named, before.astype(F32).astype(BF), preferred_element_type=F32)
    whole = jnp.dot(named, jnp.ones((LON, LON), BF), preferred_element_type=F32).astype(BF)
    r0 = lax.broadcasted_iota(jnp.int32, (NEXP * LAT, NEXP * LAT), 0)
    r1 = lax.broadcasted_iota(jnp.int32, (NEXP * LAT, NEXP * LAT), 1)
    rows_before = ((r0 // LAT == r1 // LAT) & (r1 < r0)).astype(F32).astype(BF)
    number = within + jnp.dot(rows_before, whole, preferred_element_type=F32)
    spot = jnp.full((LAT, LON), -1.0, F32)
    for m in range(NEXP):
        spot = jnp.where(member == m, number[m * LAT : (m + 1) * LAT] + float(m * CAP), spot)
    place[...] = spot

    row_no = lax.broadcasted_iota(jnp.int32, (LON, 128), 0)

    def lat_step(i, q, south, north, edges, write):
        u = ub[i]
        v = vb[i]
        for a, b in LANES:
            n = b - a
            mid = q[i, :, a:b].astype(F32)
            down = south(a, b)
            up = north(a, b)
            west = pltpu.roll(mid, 1, 0)
            east = pltpu.roll(mid, LON - 1, 0)
            rn = row_no[:, :n]
            west = jnp.where(rn == 0, edges[1, i, 0:1, a:b], west)
            east = jnp.where(rn == LON - 1, edges[0, i, 0:1, a:b], east)
            uu, vv = u[:, :n], v[:, :n]
            lon_up = jnp.where(uu > 0, west, east)
            lat_up = jnp.where(vv > 0, down, up)
            new = mid + jnp.abs(uu) * (lon_up - mid) + jnp.abs(vv) * (lat_up - mid)
            write(i, a, b, new)

    def advance(q, step, write, points):
        def row(i):
            return lambda a, b: q[i, :, a:b].astype(F32)

        def south_halo(a, b):
            return jnp.where(t == 0, 0.0, nsh[2 * step + 1, :, a:b].astype(F32))

        def north_halo(a, b):
            return jnp.where(t == NTILE - 1, 0.0, nsh[2 * step, :, a:b].astype(F32))

        edges = ewfr
        h = halo0 if step == 0 else halo1
        h[2].wait_recv()
        h[3].wait_recv()
        for n in range(2):
            both = ewr[2 * step + n].astype(F32)
            for i in range(LAT):
                ewfr[n, i] = jnp.broadcast_to(both[i : i + 1], (8, F))

        def inner(i, carry):
            lat_step(i, q, row(i - 1), row(i + 1), edges, write)
            points(i)
            return carry

        lax.fori_loop(1, LAT - 1, inner, 0)
        h[0].wait_recv()
        h[1].wait_recv()
        lat_step(0, q, south_halo, row(1), edges, write)
        lat_step(LAT - 1, q, row(LAT - 2), north_halo, edges, write)

    def write_first(i, a, b, new):
        q1[i, :, a:b] = new.astype(BF)
        put_edge(0, i, a, b, new[0:1])
        put_edge(1, i, a, b, new[LON - 1 : LON])

    def write_last(i, a, b, new):
        out = new.astype(BF)
        adv[i, :, a:b] = out
        if a == MAIN:
            xt[i, :, 0 : F - MAIN] = out

    def points_first(i):
        @pl.when(i % 4 == 3)
        def _():
            ring_point(i // 4)

    def points_last(i):
        @pl.when(i % 4 == 3)
        def _():
            ring_point(3 + i // 4)

    advance(q0, 0, write_first, points_first)
    ews[2] = ewfs[0].astype(BF)
    ews[3] = ewfs[1].astype(BF)
    for h in (halo1[2], halo1[3], halo1[0], halo1[1]):
        h.start()

    xt[...] = jnp.zeros_like(xt)

    for i in range(LAT):
        pcol[i] = jnp.transpose(jnp.broadcast_to(place[i : i + 1, :], (LON, LON)))
        tend_ref[i] = jnp.zeros((LON, OUTW), BF)

    advance(q1, 1, write_last, points_last)
    ring_point(6)
    cp_adv.start()

    def forward(k):
        return pltpu.make_async_remote_copy(
            send.at[k], recv.at[k], f_s.at[k], f_r.at[k], device_id=dest_id(k), device_id_type=MESH
        )

    def back(k):
        return pltpu.make_async_remote_copy(
            rs.at[k], rr.at[k], r_s.at[k], r_r.at[k], device_id=source_id(k), device_id_type=MESH
        )

    slot_no = lax.broadcasted_iota(jnp.int32, (CAP, LON), 0)

    def pack(gi, carry):
        for b in range(GB):
            wanted = (slot_no + dest_base(gi * GB + b)).astype(F32)
            for i in range(LAT):
                hit = place[i : i + 1, :] == wanted
                pmat[b * CAP : (b + 1) * CAP, i * LON : (i + 1) * LON] = hit.astype(F32).astype(BF)
        main = jnp.dot(
            pmat[...], adv[:, :, 0:MAIN].reshape(COLS, MAIN), preferred_element_type=F32
        )
        tail = jnp.dot(pmat[...], xt[...].reshape(COLS, 128), preferred_element_type=F32)
        for b in range(GB):
            k = gi * GB + b
            for n in range(4):
                part = main[b * CAP : (b + 1) * CAP, n * 128 : (n + 1) * 128]
                send[k, n * CAP : (n + 1) * CAP, :] = part.astype(BF)
            low = tail[b * CAP : b * CAP + CAP // 2]
            high = tail[b * CAP + CAP // 2 : (b + 1) * CAP]
            send[k, 4 * CAP : ROWS_OUT, :] = (low + pltpu.roll(high, 64, 1)).astype(BF)
            if b == 0:

                @pl.when(gi == 0)
                def _():
                    recv[0] = send[0]

                @pl.when(gi > 0)
                def _():
                    forward(k).start()
            else:
                forward(k).start()
        ring_point(ADV_POINTS + gi)
        return carry

    lax.fori_loop(0, NG, pack, 0)
    ring_points(ADV_POINTS + NG, POINTS)

    @pl.when((rel == 4) | (rel == 5))
    def _():
        def landed(k, carry):
            wcopy(k, 1, w_s1).wait_recv()
            return carry

        lax.fori_loop(0, CHUNKS, landed, 0)

    def weights(base, rows, parts):
        return jnp.concatenate(
            [wts[base + n * rows : base + (n + 1) * rows, :] for n in range(parts)], axis=1
        )

    def net(gi, carry):
        for b in range(GB):
            k = gi * GB + b
            if b == 0:

                @pl.when(gi > 0)
                def _():
                    forward(k).wait_recv()
            else:
                forward(k).wait_recv()
            for n in range(4):
                xin[b * CAP : (b + 1) * CAP, n * 128 : (n + 1) * 128] = recv[
                    k, n * CAP : (n + 1) * CAP, :
                ]
            both = recv[k, 4 * CAP : ROWS_OUT, :]
            xin[b * CAP : b * CAP + CAP // 2, MAIN:640] = both
            xin[b * CAP + CAP // 2 : (b + 1) * CAP, MAIN:640] = pltpu.roll(
                both.astype(F32), 64, 1
            ).astype(BF)
        h = jnp.dot(xin[:, 0:KIN], weights(0, KIN, 4), preferred_element_type=F32)
        h = jnp.maximum(h, 0.15 * h).astype(BF)
        for layer in range(NMID):
            w = weights(W_MID + layer * 4 * HID, HID, 4)
            h = jnp.dot(h, w, preferred_element_type=F32)
            h = jnp.maximum(h, 0.15 * h).astype(BF)
        out = jnp.dot(h, weights(W_OUT, HID, 3), preferred_element_type=F32).astype(BF)
        for b in range(GB):
            k = gi * GB + b
            for n in range(3):
                rs[k, n * CAP : (n + 1) * CAP, :] = out[
                    b * CAP : (b + 1) * CAP, n * 128 : (n + 1) * 128
                ]
            if b == 0:

                @pl.when(gi == 0)
                def _():
                    rr[0] = rs[0]

                @pl.when(gi > 0)
                def _():
                    back(k).start()
            else:
                back(k).start()
        return carry

    lax.fori_loop(0, NG, net, 0)

    lane_no = lax.broadcasted_iota(jnp.int32, (1, GB * CAP), 1)

    def unpack(gi, carry):
        blocks = []
        wanted = lane_no
        for b in range(GB):
            k = gi * GB + b
            if b == 0:

                @pl.when(gi > 0)
                def _():
                    back(k).wait_recv()
            else:
                back(k).wait_recv()
            blocks.append(
                jnp.concatenate([rr[k, n * CAP : (n + 1) * CAP, :] for n in range(3)], axis=1)
            )
            mine = (lane_no >= b * CAP) & (lane_no < (b + 1) * CAP)
            wanted = jnp.where(mine, lane_no - b * CAP + dest_base(k), wanted)
        block = jnp.concatenate(blocks, axis=0)
        wanted = wanted.astype(F32)

        def lats(i, carry):
            hits = []
            for s in range(4):
                col = pcol[i * 4 + s]
                hits.append(
                    jnp.concatenate(
                        [
                            (col == wanted[:, n * 128 : (n + 1) * 128]).astype(F32).astype(BF)
                            for n in range(3)
                        ],
                        axis=1,
                    )
                )
            got = jnp.dot(jnp.concatenate(hits, axis=0), block, preferred_element_type=F32)
            for s in range(4):
                old = tend_ref[i * 4 + s].astype(F32)
                new = old + got[s * LON : (s + 1) * LON, 0:OUTW]
                tend_ref[i * 4 + s] = new.astype(BF)
            return carry

        lax.fori_loop(0, LAT // 4, lats, 0)
        return carry

    lax.fori_loop(0, NG, unpack, 0)

    for h in halo0 + halo1:
        h.wait_send()

    def sent(k, carry):
        forward(k).wait_send()
        back(k).wait_send()
        return carry

    lax.fori_loop(1, NEXP, sent, 0)

    def passed_on(k, carry):
        wcopy(k, 1, w_s1).wait_send()
        return carry

    @pl.when((rel != 4) & (rel != 5))
    def _():
        lax.fori_loop(0, CHUNKS, passed_on, 0)

    @pl.when(rel == 0)
    def _():
        def passed_down(k, carry):
            wcopy(k, -1, w_s2).wait_send()
            return carry

        lax.fori_loop(0, CHUNKS, passed_down, 0)

    cp_adv.wait()


def on_device(state, courant, route, counts, w_in, w_mid, w_out):
    anywhere = pl.BlockSpec(memory_space=pl.ANY)
    vmem = pl.BlockSpec(memory_space=pltpu.VMEM)
    dma = pltpu.SemaphoreType.DMA
    scratch = [
        pltpu.VMEM((LAT, LON, F), BF),
        pltpu.VMEM((LAT, LON, F), BF),
        pltpu.VMEM((LAT, LON, F), BF),
        pltpu.VMEM((LAT, LON, 128), BF),
        pltpu.VMEM((LAT, LON, 2), BF),
        pltpu.VMEM((LAT, LON, 128), F32),
        pltpu.VMEM((LAT, LON, 128), F32),
        pltpu.VMEM((4, LON, F), BF),
        pltpu.VMEM((4, LAT, F), BF),
        pltpu.VMEM((4, LAT, F), BF),
        pltpu.VMEM((2, LAT, F), F32),
        pltpu.VMEM((2, LAT, 8, F), F32),
        pltpu.VMEM((LAT, LON), F32),
        pltpu.VMEM((LAT, LON, 128), F32),
        pltpu.VMEM((GB * CAP, COLS), BF),
        pltpu.VMEM((NEXP, ROWS_OUT, 128), BF),
        pltpu.VMEM((NEXP, ROWS_OUT, 128), BF),
        pltpu.VMEM((NEXP, ROWS_RET, 128), BF),
        pltpu.VMEM((NEXP, ROWS_RET, 128), BF),
        pltpu.VMEM((W_ROWS, 128), BF),
        pltpu.VMEM((1, F, HID), BF),
        pltpu.VMEM((1, NMID, HID, HID), BF),
        pltpu.VMEM((1, HID, OUTW), BF),
        pltpu.VMEM((GB * CAP, 640), BF),
        dma((6,)),
        dma((8,)),
        dma((8,)),
        dma((CHUNKS,)),
        dma((CHUNKS,)),
        dma((CHUNKS,)),
        dma((NEXP,)),
        dma((NEXP,)),
        dma((NEXP,)),
        dma((NEXP,)),
    ]
    return pl.pallas_call(
        kernel,
        out_shape=(
            jax.ShapeDtypeStruct((LAT, LON, F), BF),
            jax.ShapeDtypeStruct((LAT, LON, OUTW), BF),
        ),
        in_specs=[pl.BlockSpec(memory_space=pltpu.SMEM), vmem] + [anywhere] * 5,
        out_specs=(anywhere, vmem),
        scratch_shapes=scratch,
        compiler_params=pltpu.CompilerParams(
            collective_id=0, has_side_effects=True, vmem_limit_bytes=60 * 2**20
        ),
        name="step",
    )(counts, route.reshape(LAT, LON), state, courant, w_in, w_mid, w_out)


def solution(mesh):
    in_specs = (
        P("tile", "grp", None),
        P("tile", "grp", None),
        P("tile", "grp", None, None),
        P("tile"),
        P("tile", None, None),
        P("tile", None, None, None),
        P("tile", None, None),
    )
    out_specs = (P("tile", "grp", None), P("tile", "grp", None))
    return jax.shard_map(
        on_device, mesh=mesh, in_specs=in_specs, out_specs=out_specs, check_vma=False
    )
```

```python
import jax
import jax.numpy as jnp
from jax import lax
from jax.experimental import pallas as pl
from jax.experimental.pallas import tpu as pltpu
from jax.sharding import PartitionSpec as P

BF = jnp.bfloat16
F32 = jnp.float32
MESH = pl.DeviceIdType.MESH

F, HID, OUTW, NMID = 556, 512, 368, 3
FP = 560
FZ = 640
OUTP = 384
LAT, LON, COLS = 16, 128, 2048
CAP = 96
NEXP = 32
NTILE = 32
MAIN = 512
KIN = 576
PARTS = ((0, 256), (256, FP))
ROWS_A = 2 * CAP
ROWS_B = 2 * CAP + CAP // 2
ROWS_RET = 3 * CAP
W_MID = 4 * KIN
W_OUT = W_MID + NMID * 4 * HID
W_ROWS = W_OUT + 4 * OUTP
CHUNKS = 24
CH = W_ROWS // CHUNKS
LAG = 2
GB = 4
NG = NEXP // GB
SLOTS = GB * CAP
FIRST = 3
EARLY = 4
POINTS = CHUNKS + 3 * LAG


def transposed_dot(a, b):
    return lax.dot_general(a, b, (((1,), (1,)), ((), ())), preferred_element_type=F32)


def kernel(
    counts_hbm, route_hbm, state_hbm, cour_hbm, win_hbm, wmid_hbm, wout_hbm,
    adv_hbm, tend_hbm,
    counts_ref, route_ref, tend_ref,
    st, q32, q0, q1, adv, cour, sel, lon, nsh, xs, xr, hx, place, pall,
    send_a, recv_a, send_b, recv_b, rs, rr, wts, wi, wm, wo, xin, rt,
    lsem, hs_sem, hr_sem, w_s1, w_s2, w_r, fa_s, fa_r, fb_s, fb_r, r_s, r_r,
):
    t = lax.axis_index("tile")
    g = lax.axis_index("grp")
    y, z, x, c = t // 8, t % 8, g // 2, g % 2

    def dest(k):
        j = lax.rem(k * 13, NEXP)
        return lax.rem(y + j // 8, 4), lax.rem(x + (j // 2) % 4, 4), lax.rem(c + j % 2, 2)

    def dest_id(k):
        ty, tx, tc = dest(k)
        return {"tile": ty * 8 + z, "grp": tx * 2 + tc}

    def dest_base(k):
        ty, tx, tc = dest(k)
        return (ty * 8 + tx + 4 * tc) * CAP

    def source_id(k):
        j = lax.rem(k * 13, NEXP)
        ty = lax.rem(y + 4 - j // 8, 4)
        tx = lax.rem(x + 4 - (j // 2) % 4, 4)
        return {"tile": ty * 8 + z, "grp": tx * 2 + lax.rem(c + j % 2, 2)}

    def ring_id(d):
        return {"tile": y * 8 + lax.rem(z + d + 8, 8)}

    def tile_id(d):
        return {"tile": lax.rem(t + d + NTILE, NTILE)}

    def grp_id(d):
        return {"grp": lax.rem(g + d + 8, 8)}

    rel = lax.rem(z + 8 - (x + 4 * c), 8)
    forward_up = (rel >= 1) & (rel <= 3)
    forward_down = rel >= 6
    hop = jnp.where(rel <= 4, rel, 8 - rel)

    barrier = pltpu.get_barrier_semaphore()

    def greet(k, carry):
        pl.semaphore_signal(barrier, inc=1, device_id=dest_id(k), device_id_type=MESH)
        return carry

    lax.fori_loop(1, NEXP, greet, 0)
    for d in (1, -1):
        pl.semaphore_signal(barrier, inc=1, device_id=ring_id(d), device_id_type=MESH)
        pl.semaphore_signal(barrier, inc=1, device_id=tile_id(d), device_id_type=MESH)
        pl.semaphore_signal(barrier, inc=1, device_id=grp_id(d), device_id_type=MESH)

    cp_state = pltpu.make_async_copy(state_hbm, st, lsem.at[0])
    cp_cour = pltpu.make_async_copy(cour_hbm, cour, lsem.at[1])
    cp_wi = pltpu.make_async_copy(win_hbm, wi, lsem.at[2])
    cp_wm = pltpu.make_async_copy(wmid_hbm, wm, lsem.at[3])
    cp_wo = pltpu.make_async_copy(wout_hbm, wo, lsem.at[4])
    cp_adv = pltpu.make_async_copy(st, adv_hbm, lsem.at[5])
    cp_tend = pltpu.make_async_copy(tend_ref, tend_hbm, lsem.at[6])
    cp_counts = pltpu.make_async_copy(counts_hbm, counts_ref, lsem.at[7])
    cp_route = pltpu.make_async_copy(route_hbm, route_ref, lsem.at[8])
    cp_state.start()
    cp_cour.start()
    cp_counts.start()
    cp_route.start()

    @pl.when(rel == 0)
    def _():
        cp_wi.start()
        cp_wm.start()
        cp_wo.start()

    def halo(n, src, dst, device):
        return pltpu.make_async_remote_copy(
            src, dst, hs_sem.at[n], hr_sem.at[n], device_id=device, device_id_type=MESH
        )

    def halos(step, part, q):
        lo, hi = PARTS[part]
        own = pl.ds(lo, hi - lo)
        b = 8 * step + 4 * part
        return [
            halo(b, q.at[0, own], nsh.at[2 * step, own], tile_id(-1)),
            halo(b + 1, q.at[LAT - 1, own], nsh.at[2 * step + 1, own], tile_id(1)),
            halo(b + 2, xs.at[step, own], xr.at[2 * step + 1, own], grp_id(-1)),
            halo(b + 3, xs.at[step, own], xr.at[2 * step, own], grp_id(1)),
        ]

    halo0 = [halos(0, 0, q0), halos(0, 1, q0)]
    halo1 = [halos(1, 0, q1), halos(1, 1, q1)]

    def wcopy(k, d, sem):
        part = wts.at[pl.ds(pl.multiple_of(k * CH, CH), CH)]
        return pltpu.make_async_remote_copy(
            part, part, sem.at[k], w_r.at[k], device_id=ring_id(d), device_id_type=MESH
        )

    def ring_point(p):
        k = p - LAG * hop
        ok = (k >= 0) & (k < CHUNKS)

        @pl.when(ok & (rel == 0))
        def _():
            wcopy(k, 1, w_s1).start()
            wcopy(k, -1, w_s2).start()

        @pl.when(ok & forward_up)
        def _():
            wcopy(k, 1, w_s1).wait_recv()
            wcopy(k, 1, w_s1).start()

        @pl.when(ok & forward_down)
        def _():
            wcopy(k, -1, w_s1).wait_recv()
            wcopy(k, -1, w_s1).start()

    def ring_points(a, b):
        def one(p, carry):
            ring_point(p)
            return carry

        lax.fori_loop(a, b, one, 0)

    cp_state.wait()

    def widen(i, carry):
        for s in range(4):
            q32[pl.ds(pl.multiple_of((i * 4 + s) * LAT, LAT), LAT), :] = st[i * 4 + s].astype(F32)
        return carry

    lax.fori_loop(0, F // 4, widen, 0)
    q32[F * LAT : FP * LAT, :] = jnp.zeros(((FP - F) * LAT, LON), F32)

    for i in range(LAT):
        q0[i] = q32[pl.ds(i, FP, stride=LAT), :].astype(BF)

    s_row = lax.broadcasted_iota(jnp.int32, (LON, 128), 0)
    s_lane = lax.broadcasted_iota(jnp.int32, (LON, 128), 1)
    for i in range(LAT):
        pick = ((s_row == LON - 1) & (s_lane == i)) | ((s_row == 0) & (s_lane == 64 + i))
        sel[i * LON : (i + 1) * LON, :] = pick.astype(F32).astype(BF)

    def edges(step, part, q):
        lo, hi = PARTS[part]
        row = jnp.concatenate([q[i, lo:hi, :] for i in range(LAT)], axis=1)
        xs[step, lo:hi, :] = jnp.dot(row, sel[...], preferred_element_type=F32).astype(BF)

    edges(0, 0, q0)
    edges(0, 1, q0)

    cp_cour.wait()

    def lon_matrix(i, carry):
        u = cour[i].astype(F32)[0:1]
        pos, neg = jnp.maximum(u, 0.0), jnp.maximum(-u, 0.0)
        top = jnp.where(s_row == s_lane - 1, pos, 0.0)
        top = jnp.where(s_row == s_lane + 1, neg, top)
        top = jnp.where(s_row == s_lane, -(pos + neg), top)
        low = jnp.where((s_row == i) & (s_lane == 0), pos, 0.0)
        low = jnp.where((s_row == 64 + i) & (s_lane == LON - 1), neg, low)
        lon[i, 0:LON, :] = top.astype(BF)
        lon[i, LON : 2 * LON, :] = low.astype(BF)
        return carry

    lax.fori_loop(0, LAT, lon_matrix, 0)

    cp_counts.wait()
    cp_route.wait()

    lat_no = lax.broadcasted_iota(jnp.int32, (LAT, LON), 0)
    lon_no = lax.broadcasted_iota(jnp.int32, (LAT, LON), 1) + g * LON
    reach = jnp.zeros((LAT, LON), jnp.int32)
    for i in range(LAT):
        reach = jnp.where(lat_no == i, counts_ref[i], reach)
    member = jnp.where(lon_no < reach, route_ref[...], -1)
    named = jnp.concatenate([(member == m).astype(F32) for m in range(NEXP)], axis=0).astype(BF)
    before = (
        lax.broadcasted_iota(jnp.int32, (LON, LON), 0)
        < lax.broadcasted_iota(jnp.int32, (LON, LON), 1)
    )
    within = jnp.dot(named, before.astype(F32).astype(BF), preferred_element_type=F32)
    whole = jnp.dot(named, jnp.ones((LON, LON), BF), preferred_element_type=F32).astype(BF)
    r0 = lax.broadcasted_iota(jnp.int32, (NEXP * LAT, NEXP * LAT), 0)
    r1 = lax.broadcasted_iota(jnp.int32, (NEXP * LAT, NEXP * LAT), 1)
    rows_before = ((r0 // LAT == r1 // LAT) & (r1 < r0)).astype(F32).astype(BF)
    number = within + jnp.dot(rows_before, whole, preferred_element_type=F32)
    spot = jnp.full((LAT, LON), -1.0, F32)
    for m in range(NEXP):
        spot = jnp.where(member == m, number[m * LAT : (m + 1) * LAT] + float(m * CAP), spot)
    place[...] = spot

    slot_no = lax.broadcasted_iota(jnp.int32, (CAP, LON), 0)

    def hits(gi, carry):
        for b in range(GB):
            wanted = (slot_no + dest_base(gi * GB + b)).astype(F32)
            for i in range(LAT):
                hit = place[i : i + 1, :] == wanted
                pall[gi, b * CAP : (b + 1) * CAP, i * LON : (i + 1) * LON] = hit.astype(F32).astype(BF)
        return carry

    def lat_step(i, lo, hi, q, south, north, write):
        row = jnp.concatenate([q[i, lo:hi, :], hx[lo:hi, :]], axis=1)
        part = jnp.dot(row, lon[i], preferred_element_type=F32)
        v = cour[i].astype(F32)[1:2]
        half = (hi - lo) // 32 * 16
        for a, b in ((lo, lo + half), (lo + half, hi)):
            mid = q[i, a:b, :].astype(F32)
            lat_up = jnp.where(jnp.broadcast_to(v > 0, (b - a, LON)), south(a, b), north(a, b))
            write(i, a, b, mid + part[a - lo : b - lo] + jnp.abs(v) * (lat_up - mid))

    def advance(q, step, p, write):
        lo, hi = PARTS[p]

        def row(i):
            return lambda a, b: q[i, a:b, :].astype(F32)

        def south_halo(a, b):
            return jnp.where(t == 0, 0.0, nsh[2 * step + 1, a:b, :].astype(F32))

        def north_halo(a, b):
            return jnp.where(t == NTILE - 1, 0.0, nsh[2 * step, a:b, :].astype(F32))

        h = (halo0 if step == 0 else halo1)[p]
        h[2].wait_recv()
        h[3].wait_recv()
        west, east = xr[2 * step, lo:hi].astype(F32), xr[2 * step + 1, lo:hi].astype(F32)
        lane_no = lax.broadcasted_iota(jnp.int32, (hi - lo, 128), 1)
        hx[lo:hi, :] = jnp.where(lane_no < 64, west, east).astype(BF)

        def inner(i, carry):
            lat_step(i, lo, hi, q, row(i - 1), row(i + 1), write)
            return carry

        lax.fori_loop(1, LAT - 1, inner, 0)
        h[0].wait_recv()
        h[1].wait_recv()
        lat_step(0, lo, hi, q, south_halo, row(1), write)
        lat_step(LAT - 1, lo, hi, q, row(LAT - 2), north_halo, write)

    def write_first(i, a, b, new):
        q1[i, a:b, :] = new.astype(BF)

    def write_last(i, a, b, new):
        out = new.astype(BF)
        adv[i, a:b, :] = out
        q32[pl.ds(a * LAT + i, b - a, stride=LAT), :] = out.astype(F32)

    pl.semaphore_wait(barrier, NEXP - 1 + 6)
    for p in range(2):
        for n in (2, 3, 0, 1):
            halo0[p][n].start()

    @pl.when(rel == 0)
    def _():
        cp_wi.wait()
        cp_wm.wait()
        cp_wo.wait()
        for n in range(4):
            wts[n * KIN + 544 : (n + 1) * KIN, :] = jnp.zeros((KIN - 544, 128), BF)
            wts[n * KIN : n * KIN + F, :] = wi[0, :, n * 128 : (n + 1) * 128]
        for k in range(NMID):
            for n in range(4):
                r = W_MID + (k * 4 + n) * HID
                wts[r : r + HID, :] = wm[0, k, :, n * 128 : (n + 1) * 128]
        for n in range(4):
            r = W_OUT + n * OUTP
            wts[r : r + OUTW, :] = wo[0, :, n * 128 : (n + 1) * 128]
            wts[r + OUTW : r + OUTP, :] = jnp.zeros((OUTP - OUTW, 128), BF)

    lax.fori_loop(0, NG, hits, 0)
    for i in range(LAT):
        adv[i, FP:FZ, :] = jnp.zeros((FZ - FP, LON), BF)
        tend_ref[i] = jnp.zeros((OUTW, LON), BF)
    for p in range(2):
        advance(q0, 0, p, write_first)
        halo1[p][0].start()
        halo1[p][1].start()
        edges(1, p, q1)
        halo1[p][2].start()
        halo1[p][3].start()
        ring_point(p)

    def forward(p, k):
        src, dst, s_sem, r_sem = ((send_a, recv_a, fa_s, fa_r), (send_b, recv_b, fb_s, fb_r))[p]
        return pltpu.make_async_remote_copy(
            src.at[k], dst.at[k], s_sem.at[k], r_sem.at[k], device_id=dest_id(k), device_id_type=MESH
        )

    def back(k):
        return pltpu.make_async_remote_copy(
            rs.at[k], rr.at[k], r_s.at[k], r_r.at[k], device_id=source_id(k), device_id_type=MESH
        )

    def launch(p, gi, b):
        k = gi * GB + b
        if b > 0:
            forward(p, k).start()
            return

        @pl.when(gi == 0)
        def _():
            if p == 0:
                recv_a[0] = send_a[0]
            else:
                recv_b[0] = send_b[0]

        @pl.when(gi > 0)
        def _():
            forward(p, k).start()

    def pack_a(gi, carry):
        columns = jnp.concatenate([adv[i, 0:256, :] for i in range(LAT)], axis=1)
        rows = transposed_dot(pall[gi], columns)
        for b in range(GB):
            for n in range(2):
                part = rows[b * CAP : (b + 1) * CAP, n * 128 : (n + 1) * 128]
                send_a[gi * GB + b, n * CAP : (n + 1) * CAP, :] = part.astype(BF)
            launch(0, gi, b)
        ring_point(jnp.where(gi < FIRST, EARLY - 1, EARLY) + gi)
        return carry

    def pack_b(gi, carry):
        columns = jnp.concatenate([adv[i, 256:FZ, :] for i in range(LAT)], axis=1)
        rows = transposed_dot(pall[gi], columns)
        for b in range(GB):
            for n in range(2):
                part = rows[b * CAP : (b + 1) * CAP, n * 128 : (n + 1) * 128]
                send_b[gi * GB + b, n * CAP : (n + 1) * CAP, :] = part.astype(BF)
            low = rows[b * CAP : b * CAP + CAP // 2, 256:384]
            high = rows[b * CAP + CAP // 2 : (b + 1) * CAP, 256:384]
            send_b[gi * GB + b, 2 * CAP : ROWS_B, :] = (low + pltpu.roll(high, 64, 1)).astype(BF)
            launch(1, gi, b)
        ring_point(EARLY + NG + gi)
        return carry

    advance(q1, 1, 0, write_last)
    ring_point(2)
    lax.fori_loop(0, FIRST, pack_a, 0)
    advance(q1, 1, 1, write_last)
    ring_point(EARLY - 1 + FIRST)
    lax.fori_loop(FIRST, NG, pack_a, 0)
    lax.fori_loop(0, NG, pack_b, 0)

    def narrow(i, carry):
        for s in range(4):
            st[i * 4 + s] = q32[pl.ds(pl.multiple_of((i * 4 + s) * LAT, LAT), LAT), :].astype(BF)
        return carry

    lax.fori_loop(0, F // 4, narrow, 0)
    cp_adv.start()
    ring_points(EARLY + 2 * NG, POINTS)

    @pl.when((rel == 4) | (rel == 5))
    def _():
        def landed(k, carry):
            wcopy(k, 1, w_s1).wait_recv()
            return carry

        lax.fori_loop(0, CHUNKS, landed, 0)

    def weights(base, rows, parts):
        return jnp.concatenate(
            [wts[base + n * rows : base + (n + 1) * rows, :] for n in range(parts)], axis=1
        )

    def net(gi, carry):
        for b in range(GB):
            k = gi * GB + b
            if b == 0:

                @pl.when(gi > 0)
                def _():
                    forward(0, k).wait_recv()
                    forward(1, k).wait_recv()
            else:
                forward(0, k).wait_recv()
                forward(1, k).wait_recv()
            own = slice(b * CAP, (b + 1) * CAP)
            for n in range(2):
                xin[own, n * 128 : (n + 1) * 128] = recv_a[k, n * CAP : (n + 1) * CAP, :]
                xin[own, 256 + n * 128 : 384 + n * 128] = recv_b[k, n * CAP : (n + 1) * CAP, :]
            both = recv_b[k, 2 * CAP : ROWS_B, :]
            xin[b * CAP : b * CAP + CAP // 2, MAIN:640] = both
            xin[b * CAP + CAP // 2 : (b + 1) * CAP, MAIN:640] = pltpu.roll(
                both.astype(F32), 64, 1
            ).astype(BF)
        h = jnp.dot(xin[:, 0:KIN], weights(0, KIN, 4), preferred_element_type=F32)
        h = jnp.maximum(h, 0.15 * h).astype(BF)
        for layer in range(NMID):
            w = weights(W_MID + layer * 4 * HID, HID, 4)
            h = jnp.dot(h, w, preferred_element_type=F32)
            h = jnp.maximum(h, 0.15 * h).astype(BF)
        out = transposed_dot(h, weights(W_OUT, OUTP, 4)).astype(BF)
        for b in range(GB):
            k = gi * GB + b
            for n in range(3):
                rs[k, n * CAP : (n + 1) * CAP, :] = out[
                    b * CAP : (b + 1) * CAP, n * 128 : (n + 1) * 128
                ]
            if b == 0:

                @pl.when(gi == 0)
                def _():
                    rr[0] = rs[0]

                @pl.when(gi > 0)
                def _():
                    back(k).start()
            else:
                back(k).start()
        return carry

    lax.fori_loop(0, NG, net, 0)

    def unpack(gi, carry):
        for b in range(GB):
            k = gi * GB + b
            if b == 0:

                @pl.when(gi > 0)
                def _():
                    back(k).wait_recv()
            else:
                back(k).wait_recv()
        block = jnp.concatenate(
            [
                jnp.concatenate(
                    [rr[gi * GB + b, n * CAP : (n + 1) * CAP, :] for n in range(3)], axis=1
                )
                for b in range(GB)
            ],
            axis=0,
        )
        rt[...] = jnp.transpose(block.astype(F32)).astype(BF)[0:OUTW]
        for i in range(0, LAT, 4):
            got = jnp.dot(
                rt[...], pall[gi, :, i * LON : (i + 4) * LON], preferred_element_type=F32
            )
            for s in range(4):
                old = tend_ref[i + s].astype(F32)
                tend_ref[i + s] = (old + got[:, s * LON : (s + 1) * LON]).astype(BF)
        return carry

    lax.fori_loop(0, NG, unpack, 0)

    cp_tend.start()
    for hs in halo0 + halo1:
        for h in hs:
            h.wait_send()

    def sent(k, carry):
        forward(0, k).wait_send()
        forward(1, k).wait_send()
        back(k).wait_send()
        return carry

    lax.fori_loop(1, NEXP, sent, 0)

    def passed_on(k, carry):
        wcopy(k, 1, w_s1).wait_send()
        return carry

    @pl.when((rel != 4) & (rel != 5))
    def _():
        lax.fori_loop(0, CHUNKS, passed_on, 0)

    @pl.when(rel == 0)
    def _():
        def passed_down(k, carry):
            wcopy(k, -1, w_s2).wait_send()
            return carry

        lax.fori_loop(0, CHUNKS, passed_down, 0)

    cp_adv.wait()
    cp_tend.wait()


def copy_kernel(adv_in, tend_in, adv_out, tend_out, adv_v, tend_v, sem_in, sem_out):
    into, out = [], []
    for j, (a, v, b, n) in enumerate(
        ((adv_in, adv_v, adv_out, F // 4), (tend_in, tend_v, tend_out, LAT // 4))
    ):
        for i in range(4):
            part = pl.ds(i * n, n)
            into.append(pltpu.make_async_copy(a.at[part], v.at[part], sem_in.at[4 * j + i]))
            out.append(pltpu.make_async_copy(v.at[part], b.at[part], sem_out.at[4 * j + i]))
    for one in into:
        one.start()
    for one, two in zip(into, out):
        one.wait()
        two.start()
    for two in out:
        two.wait()


def on_device(state, courant, route, counts, w_in, w_mid, w_out):
    anywhere = pl.BlockSpec(memory_space=pl.ANY)
    dma = pltpu.SemaphoreType.DMA
    scratch = [
        pltpu.SMEM((LAT,), jnp.int32),
        pltpu.VMEM((LAT, LON), jnp.int32),
        pltpu.VMEM((LAT, OUTW, LON), BF),
        pltpu.VMEM((F, LAT, LON), BF),
        pltpu.VMEM((FP * LAT, LON), F32),
        pltpu.VMEM((LAT, FP, LON), BF),
        pltpu.VMEM((LAT, FP, LON), BF),
        pltpu.VMEM((LAT, FZ, LON), BF),
        pltpu.VMEM((LAT, 2, LON), BF),
        pltpu.VMEM((COLS, 128), BF),
        pltpu.VMEM((LAT, 2 * LON, LON), BF),
        pltpu.VMEM((4, FP, LON), BF),
        pltpu.VMEM((2, FP, 128), BF),
        pltpu.VMEM((4, FP, 128), BF),
        pltpu.VMEM((FP, 128), BF),
        pltpu.VMEM((LAT, LON), F32),
        pltpu.VMEM((NG, SLOTS, COLS), BF),
        pltpu.VMEM((NEXP, ROWS_A, 128), BF),
        pltpu.VMEM((NEXP, ROWS_A, 128), BF),
        pltpu.VMEM((NEXP, ROWS_B, 128), BF),
        pltpu.VMEM((NEXP, ROWS_B, 128), BF),
        pltpu.VMEM((NEXP, ROWS_RET, 128), BF),
        pltpu.VMEM((NEXP, ROWS_RET, 128), BF),
        pltpu.VMEM((W_ROWS, 128), BF),
        pltpu.VMEM((1, F, HID), BF),
        pltpu.VMEM((1, NMID, HID, HID), BF),
        pltpu.VMEM((1, OUTW, HID), BF),
        pltpu.VMEM((SLOTS, FZ), BF),
        pltpu.VMEM((OUTW, SLOTS), BF),
        dma((9,)),
        dma((16,)),
        dma((16,)),
        dma((CHUNKS,)),
        dma((CHUNKS,)),
        dma((CHUNKS,)),
        dma((NEXP,)),
        dma((NEXP,)),
        dma((NEXP,)),
        dma((NEXP,)),
        dma((NEXP,)),
        dma((NEXP,)),
    ]
    adv, tend = pl.pallas_call(
        kernel,
        out_shape=(
            jax.ShapeDtypeStruct((F, LAT, LON), BF),
            jax.ShapeDtypeStruct((LAT, OUTW, LON), BF),
        ),
        in_specs=[anywhere] * 7,
        out_specs=(anywhere, anywhere),
        scratch_shapes=scratch,
        compiler_params=pltpu.CompilerParams(
            collective_id=0, has_side_effects=True, vmem_limit_bytes=60 * 2**20
        ),
        name="step",
    )(
        counts,
        route.reshape(LAT, LON),
        jnp.transpose(state, (2, 0, 1)),
        jnp.transpose(courant, (0, 2, 1)),
        w_in,
        w_mid,
        jnp.transpose(w_out, (0, 2, 1)),
    )
    adv, tend = pl.pallas_call(
        copy_kernel,
        out_shape=(
            jax.ShapeDtypeStruct(adv.shape, BF),
            jax.ShapeDtypeStruct(tend.shape, BF),
        ),
        in_specs=[anywhere] * 2,
        out_specs=(anywhere, anywhere),
        scratch_shapes=[
            pltpu.VMEM(adv.shape, BF),
            pltpu.VMEM(tend.shape, BF),
            dma((8,)),
            dma((8,)),
        ],
        name="hand_over",
    )(adv, tend)
    return jnp.transpose(adv, (1, 2, 0)), jnp.transpose(tend, (0, 2, 1))


def solution(mesh):
    in_specs = (
        P("tile", "grp", None),
        P("tile", "grp", None),
        P("tile", "grp", None, None),
        P("tile"),
        P("tile", None, None),
        P("tile", None, None, None),
        P("tile", None, None),
    )
    out_specs = (P("tile", "grp", None), P("tile", "grp", None))
    return jax.shard_map(
        on_device, mesh=mesh, in_specs=in_specs, out_specs=out_specs, check_vma=False
    )
```

```python
import jax
import jax.numpy as jnp
from jax import lax
from jax.experimental import pallas as pl
from jax.experimental.pallas import tpu as pltpu
from jax.sharding import PartitionSpec as P

BF = jnp.bfloat16
F32 = jnp.float32
MESH = pl.DeviceIdType.MESH

F, HID, OUTW, NMID = 556, 512, 368, 3
FP = 560
FZ = 640
OUTP = 384
LAT, LON, COLS = 16, 128, 2048
CAP = 96
NEXP = 32
NTILE = 32
MAIN = 512
KIN = 576
PARTS = ((0, 256), (256, FP))
ROWS_A = 2 * CAP
ROWS_B = 2 * CAP + CAP // 2
ROWS_RET = 3 * CAP
W_MID = 4 * KIN
W_OUT = W_MID + NMID * 4 * HID
W_ROWS = W_OUT + 4 * OUTP
CHUNKS = 24
CH = W_ROWS // CHUNKS
AHEAD = 3
T_CHUNK, T_HOP, T_RELAY = 12, 52, 175
GB = 4
NG = NEXP // GB
SLOTS = GB * CAP
FIRST = 3


def transposed_dot(a, b):
    return lax.dot_general(a, b, (((1,), (1,)), ((), ())), preferred_element_type=F32)


def kernel(
    counts_hbm, route_hbm, state_hbm, cour_hbm, win_hbm, wmid_hbm, wout_hbm,
    adv_hbm, tend_hbm,
    counts_ref, route_ref, tend_ref,
    st, q32, q0, q1, adv, cour, sel, lon, nsh, xs, xr, hx, place, pall,
    send_a, recv_a, send_b, recv_b, rs, rr, wts, wi, wm, wo, xin, rt,
    lsem, hs_sem, hr_sem, w_s1, w_s2, w_r, fa_s, fa_r, fb_s, fb_r, r_s, r_r,
):
    t = lax.axis_index("tile")
    g = lax.axis_index("grp")
    y, z, x, c = t // 8, t % 8, g // 2, g % 2

    def dest(k):
        j = lax.rem(k * 13, NEXP)
        return lax.rem(y + j // 8, 4), lax.rem(x + (j // 2) % 4, 4), lax.rem(c + j % 2, 2)

    def dest_id(k):
        ty, tx, tc = dest(k)
        return {"tile": ty * 8 + z, "grp": tx * 2 + tc}

    def dest_base(k):
        ty, tx, tc = dest(k)
        return (ty * 8 + tx + 4 * tc) * CAP

    def source_id(k):
        j = lax.rem(k * 13, NEXP)
        ty = lax.rem(y + 4 - j // 8, 4)
        tx = lax.rem(x + 4 - (j // 2) % 4, 4)
        return {"tile": ty * 8 + z, "grp": tx * 2 + lax.rem(c + j % 2, 2)}

    def ring_id(d):
        return {"tile": y * 8 + lax.rem(z + d + 8, 8)}

    def tile_id(d):
        return {"tile": lax.rem(t + d + NTILE, NTILE)}

    def grp_id(d):
        return {"grp": lax.rem(g + d + 8, 8)}

    rel = lax.rem(z + 8 - (x + 4 * c), 8)
    forward_up = (rel >= 1) & (rel <= 3)
    forward_down = rel >= 6
    hop = jnp.where(rel <= 4, rel, 8 - rel)

    barrier = pltpu.get_barrier_semaphore()

    def greet(k, carry):
        pl.semaphore_signal(barrier, inc=1, device_id=dest_id(k), device_id_type=MESH)
        return carry

    lax.fori_loop(1, NEXP, greet, 0)
    for d in (1, -1):
        pl.semaphore_signal(barrier, inc=1, device_id=ring_id(d), device_id_type=MESH)
        pl.semaphore_signal(barrier, inc=1, device_id=tile_id(d), device_id_type=MESH)
        pl.semaphore_signal(barrier, inc=1, device_id=grp_id(d), device_id_type=MESH)

    cp_state = pltpu.make_async_copy(state_hbm, st, lsem.at[0])
    cp_cour = pltpu.make_async_copy(cour_hbm, cour, lsem.at[1])
    cp_wi = pltpu.make_async_copy(win_hbm, wi, lsem.at[2])
    cp_wm = pltpu.make_async_copy(wmid_hbm, wm, lsem.at[3])
    cp_wo = pltpu.make_async_copy(wout_hbm, wo, lsem.at[4])
    cp_adv = pltpu.make_async_copy(st, adv_hbm, lsem.at[5])
    cp_tend = pltpu.make_async_copy(tend_ref, tend_hbm, lsem.at[6])
    cp_counts = pltpu.make_async_copy(counts_hbm, counts_ref, lsem.at[7])
    cp_route = pltpu.make_async_copy(route_hbm, route_ref, lsem.at[8])
    cp_state.start()
    cp_cour.start()
    cp_counts.start()
    cp_route.start()

    @pl.when(rel == 0)
    def _():
        cp_wi.start()
        cp_wm.start()
        cp_wo.start()

    def halo(n, src, dst, device):
        return pltpu.make_async_remote_copy(
            src, dst, hs_sem.at[n], hr_sem.at[n], device_id=device, device_id_type=MESH
        )

    def halos(step, part, q):
        lo, hi = PARTS[part]
        own = pl.ds(lo, hi - lo)
        b = 8 * step + 4 * part
        return [
            halo(b, q.at[0, own], nsh.at[2 * step, own], tile_id(-1)),
            halo(b + 1, q.at[LAT - 1, own], nsh.at[2 * step + 1, own], tile_id(1)),
            halo(b + 2, xs.at[step, own], xr.at[2 * step + 1, own], grp_id(-1)),
            halo(b + 3, xs.at[step, own], xr.at[2 * step, own], grp_id(1)),
        ]

    halo0 = [halos(0, 0, q0), halos(0, 1, q0)]
    halo1 = [halos(1, 0, q1), halos(1, 1, q1)]

    def wcopy(k, d, sem):
        part = wts.at[pl.ds(pl.multiple_of(k * CH, CH), CH)]
        return pltpu.make_async_remote_copy(
            part, part, sem.at[k], w_r.at[k], device_id=ring_id(d), device_id_type=MESH
        )

    def pass_on(k, carry):
        @pl.when(rel == 0)
        def _():
            wcopy(k, 1, w_s1).start()
            wcopy(k, -1, w_s2).start()

        @pl.when(forward_up)
        def _():
            wcopy(k, 1, w_s1).wait_recv()
            wcopy(k, 1, w_s1).start()

        @pl.when(forward_down)
        def _():
            wcopy(k, -1, w_s1).wait_recv()
            wcopy(k, -1, w_s1).start()

        return carry

    def passed_by(clock):
        behind = clock - T_RELAY - T_HOP * (hop - 1)
        relayed = jnp.where(behind < 0, 0, jnp.minimum(AHEAD + behind // T_CHUNK, CHUNKS))
        begun = jnp.where(clock >= 40, AHEAD, 0)
        begun = jnp.where(clock >= 90, 11, begun)
        begun = jnp.where(clock >= 170, 18, begun)
        begun = jnp.where(clock >= 210, CHUNKS, begun)
        return jnp.where(rel == 0, begun, jnp.where(forward_up | forward_down, relayed, 0))

    def ring(before, now):
        lax.fori_loop(passed_by(before), passed_by(now), pass_on, 0)

    cp_state.wait()

    def widen(i, carry):
        for s in range(4):
            q32[pl.ds(pl.multiple_of((i * 4 + s) * LAT, LAT), LAT), :] = st[i * 4 + s].astype(F32)
        return carry

    lax.fori_loop(0, F // 4, widen, 0)
    q32[F * LAT : FP * LAT, :] = jnp.zeros(((FP - F) * LAT, LON), F32)

    for i in range(LAT):
        q0[i] = q32[pl.ds(i, FP, stride=LAT), :].astype(BF)

    s_row = lax.broadcasted_iota(jnp.int32, (LON, 128), 0)
    s_lane = lax.broadcasted_iota(jnp.int32, (LON, 128), 1)
    for i in range(LAT):
        pick = ((s_row == LON - 1) & (s_lane == i)) | ((s_row == 0) & (s_lane == 64 + i))
        sel[i * LON : (i + 1) * LON, :] = pick.astype(F32).astype(BF)

    def edges(step, part, q):
        lo, hi = PARTS[part]
        row = jnp.concatenate([q[i, lo:hi, :] for i in range(LAT)], axis=1)
        xs[step, lo:hi, :] = jnp.dot(row, sel[...], preferred_element_type=F32).astype(BF)

    edges(0, 0, q0)
    edges(0, 1, q0)

    cp_cour.wait()

    def lon_matrix(i, carry):
        u = cour[i].astype(F32)[0:1]
        pos, neg = jnp.maximum(u, 0.0), jnp.maximum(-u, 0.0)
        top = jnp.where(s_row == s_lane - 1, pos, 0.0)
        top = jnp.where(s_row == s_lane + 1, neg, top)
        top = jnp.where(s_row == s_lane, -(pos + neg), top)
        low = jnp.where((s_row == i) & (s_lane == 0), pos, 0.0)
        low = jnp.where((s_row == 64 + i) & (s_lane == LON - 1), neg, low)
        lon[i, 0:LON, :] = top.astype(BF)
        lon[i, LON : 2 * LON, :] = low.astype(BF)
        return carry

    lax.fori_loop(0, LAT, lon_matrix, 0)

    cp_counts.wait()
    cp_route.wait()

    lat_no = lax.broadcasted_iota(jnp.int32, (LAT, LON), 0)
    lon_no = lax.broadcasted_iota(jnp.int32, (LAT, LON), 1) + g * LON
    reach = jnp.zeros((LAT, LON), jnp.int32)
    for i in range(LAT):
        reach = jnp.where(lat_no == i, counts_ref[i], reach)
    member = jnp.where(lon_no < reach, route_ref[...], -1)
    named = jnp.concatenate([(member == m).astype(F32) for m in range(NEXP)], axis=0).astype(BF)
    before = (
        lax.broadcasted_iota(jnp.int32, (LON, LON), 0)
        < lax.broadcasted_iota(jnp.int32, (LON, LON), 1)
    )
    within = jnp.dot(named, before.astype(F32).astype(BF), preferred_element_type=F32)
    whole = jnp.dot(named, jnp.ones((LON, LON), BF), preferred_element_type=F32).astype(BF)
    r0 = lax.broadcasted_iota(jnp.int32, (NEXP * LAT, NEXP * LAT), 0)
    r1 = lax.broadcasted_iota(jnp.int32, (NEXP * LAT, NEXP * LAT), 1)
    rows_before = ((r0 // LAT == r1 // LAT) & (r1 < r0)).astype(F32).astype(BF)
    number = within + jnp.dot(rows_before, whole, preferred_element_type=F32)
    spot = jnp.full((LAT, LON), -1.0, F32)
    for m in range(NEXP):
        spot = jnp.where(member == m, number[m * LAT : (m + 1) * LAT] + float(m * CAP), spot)
    place[...] = spot

    slot_no = lax.broadcasted_iota(jnp.int32, (CAP, LON), 0)

    def hits(gi, carry):
        for b in range(GB):
            wanted = (slot_no + dest_base(gi * GB + b)).astype(F32)
            for i in range(LAT):
                hit = place[i : i + 1, :] == wanted
                pall[gi, b * CAP : (b + 1) * CAP, i * LON : (i + 1) * LON] = hit.astype(F32).astype(BF)
        return carry

    def lat_step(i, lo, hi, q, south, north, write):
        row = jnp.concatenate([q[i, lo:hi, :], hx[lo:hi, :]], axis=1)
        part = jnp.dot(row, lon[i], preferred_element_type=F32)
        v = cour[i].astype(F32)[1:2]
        half = (hi - lo) // 32 * 16
        for a, b in ((lo, lo + half), (lo + half, hi)):
            mid = q[i, a:b, :].astype(F32)
            lat_up = jnp.where(jnp.broadcast_to(v > 0, (b - a, LON)), south(a, b), north(a, b))
            write(i, a, b, mid + part[a - lo : b - lo] + jnp.abs(v) * (lat_up - mid))

    def advance(q, step, p, write):
        lo, hi = PARTS[p]

        def row(i):
            return lambda a, b: q[i, a:b, :].astype(F32)

        def south_halo(a, b):
            return jnp.where(t == 0, 0.0, nsh[2 * step + 1, a:b, :].astype(F32))

        def north_halo(a, b):
            return jnp.where(t == NTILE - 1, 0.0, nsh[2 * step, a:b, :].astype(F32))

        h = (halo0 if step == 0 else halo1)[p]
        h[2].wait_recv()
        h[3].wait_recv()
        west, east = xr[2 * step, lo:hi].astype(F32), xr[2 * step + 1, lo:hi].astype(F32)
        lane_no = lax.broadcasted_iota(jnp.int32, (hi - lo, 128), 1)
        hx[lo:hi, :] = jnp.where(lane_no < 64, west, east).astype(BF)

        def inner(i, carry):
            lat_step(i, lo, hi, q, row(i - 1), row(i + 1), write)
            return carry

        lax.fori_loop(1, LAT - 1, inner, 0)
        h[0].wait_recv()
        h[1].wait_recv()
        lat_step(0, lo, hi, q, south_halo, row(1), write)
        lat_step(LAT - 1, lo, hi, q, row(LAT - 2), north_halo, write)

    def write_first(i, a, b, new):
        q1[i, a:b, :] = new.astype(BF)

    def write_last(i, a, b, new):
        out = new.astype(BF)
        adv[i, a:b, :] = out
        q32[pl.ds(a * LAT + i, b - a, stride=LAT), :] = out.astype(F32)

    pl.semaphore_wait(barrier, NEXP - 1 + 6)
    for p in range(2):
        for n in (2, 3, 0, 1):
            halo0[p][n].start()

    @pl.when(rel == 0)
    def _():
        cp_wi.wait()
        cp_wm.wait()
        cp_wo.wait()
        for n in range(4):
            wts[n * KIN + 544 : (n + 1) * KIN, :] = jnp.zeros((KIN - 544, 128), BF)
            wts[n * KIN : n * KIN + F, :] = wi[0, :, n * 128 : (n + 1) * 128]
        for k in range(NMID):
            for n in range(4):
                r = W_MID + (k * 4 + n) * HID
                wts[r : r + HID, :] = wm[0, k, :, n * 128 : (n + 1) * 128]
        for n in range(4):
            r = W_OUT + n * OUTP
            wts[r : r + OUTW, :] = wo[0, :, n * 128 : (n + 1) * 128]
            wts[r + OUTW : r + OUTP, :] = jnp.zeros((OUTP - OUTW, 128), BF)

    lax.fori_loop(0, NG, hits, 0)
    for i in range(LAT):
        adv[i, FP:FZ, :] = jnp.zeros((FZ - FP, LON), BF)
        tend_ref[i] = jnp.zeros((OUTW, LON), BF)
    ring(0, 40)
    for p in range(2):
        advance(q0, 0, p, write_first)
        halo1[p][0].start()
        halo1[p][1].start()
        edges(1, p, q1)
        halo1[p][2].start()
        halo1[p][3].start()
        ring((40, 65)[p], (65, 90)[p])

    def forward(p, k):
        src, dst, s_sem, r_sem = ((send_a, recv_a, fa_s, fa_r), (send_b, recv_b, fb_s, fb_r))[p]
        return pltpu.make_async_remote_copy(
            src.at[k], dst.at[k], s_sem.at[k], r_sem.at[k], device_id=dest_id(k), device_id_type=MESH
        )

    def back(k):
        return pltpu.make_async_remote_copy(
            rs.at[k], rr.at[k], r_s.at[k], r_r.at[k], device_id=source_id(k), device_id_type=MESH
        )

    def launch(p, gi, b):
        k = gi * GB + b
        if b > 0:
            forward(p, k).start()
            return

        @pl.when(gi == 0)
        def _():
            if p == 0:
                recv_a[0] = send_a[0]
            else:
                recv_b[0] = send_b[0]

        @pl.when(gi > 0)
        def _():
            forward(p, k).start()

    def pack_a(gi, carry):
        columns = jnp.concatenate([adv[i, 0:256, :] for i in range(LAT)], axis=1)
        rows = transposed_dot(pall[gi], columns)
        for b in range(GB):
            for n in range(2):
                part = rows[b * CAP : (b + 1) * CAP, n * 128 : (n + 1) * 128]
                send_a[gi * GB + b, n * CAP : (n + 1) * CAP, :] = part.astype(BF)
            launch(0, gi, b)
        start = jnp.where(gi < FIRST, 170, 180) + 8 * gi
        ring(start, start + 8)
        return carry

    def pack_b(gi, carry):
        columns = jnp.concatenate([adv[i, 256:FZ, :] for i in range(LAT)], axis=1)
        rows = transposed_dot(pall[gi], columns)
        for b in range(GB):
            for n in range(2):
                part = rows[b * CAP : (b + 1) * CAP, n * 128 : (n + 1) * 128]
                send_b[gi * GB + b, n * CAP : (n + 1) * CAP, :] = part.astype(BF)
            low = rows[b * CAP : b * CAP + CAP // 2, 256:384]
            high = rows[b * CAP + CAP // 2 : (b + 1) * CAP, 256:384]
            send_b[gi * GB + b, 2 * CAP : ROWS_B, :] = (low + pltpu.roll(high, 64, 1)).astype(BF)
            launch(1, gi, b)
        ring(244 + 10 * gi, 254 + 10 * gi)
        return carry

    advance(q1, 1, 0, write_last)
    ring(90, 170)
    lax.fori_loop(0, FIRST, pack_a, 0)
    advance(q1, 1, 1, write_last)
    ring(170 + 8 * FIRST, 180 + 8 * FIRST)
    lax.fori_loop(FIRST, NG, pack_a, 0)
    lax.fori_loop(0, NG, pack_b, 0)

    def narrow(i, carry):
        for s in range(4):
            st[i * 4 + s] = q32[pl.ds(pl.multiple_of((i * 4 + s) * LAT, LAT), LAT), :].astype(BF)
        return carry

    lax.fori_loop(0, F // 4, narrow, 0)
    cp_adv.start()
    ring(244 + 10 * NG, 2000)

    @pl.when((rel == 4) | (rel == 5))
    def _():
        def landed(k, carry):
            wcopy(k, 1, w_s1).wait_recv()
            return carry

        lax.fori_loop(0, CHUNKS, landed, 0)

    def weights(base, rows, parts):
        return jnp.concatenate(
            [wts[base + n * rows : base + (n + 1) * rows, :] for n in range(parts)], axis=1
        )

    def net(gi, carry):
        for b in range(GB):
            k = gi * GB + b
            if b == 0:

                @pl.when(gi > 0)
                def _():
                    forward(0, k).wait_recv()
                    forward(1, k).wait_recv()
            else:
                forward(0, k).wait_recv()
                forward(1, k).wait_recv()
            own = slice(b * CAP, (b + 1) * CAP)
            for n in range(2):
                xin[own, n * 128 : (n + 1) * 128] = recv_a[k, n * CAP : (n + 1) * CAP, :]
                xin[own, 256 + n * 128 : 384 + n * 128] = recv_b[k, n * CAP : (n + 1) * CAP, :]
            both = recv_b[k, 2 * CAP : ROWS_B, :]
            xin[b * CAP : b * CAP + CAP // 2, MAIN:640] = both
            xin[b * CAP + CAP // 2 : (b + 1) * CAP, MAIN:640] = pltpu.roll(
                both.astype(F32), 64, 1
            ).astype(BF)
        h = jnp.dot(xin[:, 0:KIN], weights(0, KIN, 4), preferred_element_type=F32)
        h = jnp.maximum(h, 0.15 * h).astype(BF)
        for layer in range(NMID):
            w = weights(W_MID + layer * 4 * HID, HID, 4)
            h = jnp.dot(h, w, preferred_element_type=F32)
            h = jnp.maximum(h, 0.15 * h).astype(BF)
        out = transposed_dot(h, weights(W_OUT, OUTP, 4)).astype(BF)
        for b in range(GB):
            k = gi * GB + b
            for n in range(3):
                rs[k, n * CAP : (n + 1) * CAP, :] = out[
                    b * CAP : (b + 1) * CAP, n * 128 : (n + 1) * 128
                ]
            if b == 0:

                @pl.when(gi == 0)
                def _():
                    rr[0] = rs[0]

                @pl.when(gi > 0)
                def _():
                    back(k).start()
            else:
                back(k).start()
        return carry

    lax.fori_loop(0, NG, net, 0)

    def unpack(gi, carry):
        for b in range(GB):
            k = gi * GB + b
            if b == 0:

                @pl.when(gi > 0)
                def _():
                    back(k).wait_recv()
            else:
                back(k).wait_recv()
        block = jnp.concatenate(
            [
                jnp.concatenate(
                    [rr[gi * GB + b, n * CAP : (n + 1) * CAP, :] for n in range(3)], axis=1
                )
                for b in range(GB)
            ],
            axis=0,
        )
        rt[...] = jnp.transpose(block.astype(F32)).astype(BF)[0:OUTW]
        for i in range(0, LAT, 4):
            got = jnp.dot(
                rt[...], pall[gi, :, i * LON : (i + 4) * LON], preferred_element_type=F32
            )
            for s in range(4):
                old = tend_ref[i + s].astype(F32)
                tend_ref[i + s] = (old + got[:, s * LON : (s + 1) * LON]).astype(BF)
        return carry

    lax.fori_loop(0, NG, unpack, 0)

    cp_tend.start()
    for hs in halo0 + halo1:
        for h in hs:
            h.wait_send()

    def sent(k, carry):
        forward(0, k).wait_send()
        forward(1, k).wait_send()
        back(k).wait_send()
        return carry

    lax.fori_loop(1, NEXP, sent, 0)

    def passed_on(k, carry):
        wcopy(k, 1, w_s1).wait_send()
        return carry

    @pl.when((rel != 4) & (rel != 5))
    def _():
        lax.fori_loop(0, CHUNKS, passed_on, 0)

    @pl.when(rel == 0)
    def _():
        def passed_down(k, carry):
            wcopy(k, -1, w_s2).wait_send()
            return carry

        lax.fori_loop(0, CHUNKS, passed_down, 0)

    cp_adv.wait()
    cp_tend.wait()


def copy_kernel(adv_in, tend_in, adv_out, tend_out, adv_v, tend_v, sem_in, sem_out):
    into, out = [], []
    for j, (a, v, b, n) in enumerate(
        ((adv_in, adv_v, adv_out, F // 4), (tend_in, tend_v, tend_out, LAT // 4))
    ):
        for i in range(4):
            part = pl.ds(i * n, n)
            into.append(pltpu.make_async_copy(a.at[part], v.at[part], sem_in.at[4 * j + i]))
            out.append(pltpu.make_async_copy(v.at[part], b.at[part], sem_out.at[4 * j + i]))
    for one in into:
        one.start()
    for one, two in zip(into, out):
        one.wait()
        two.start()
    for two in out:
        two.wait()


def on_device(state, courant, route, counts, w_in, w_mid, w_out):
    anywhere = pl.BlockSpec(memory_space=pl.ANY)
    dma = pltpu.SemaphoreType.DMA
    scratch = [
        pltpu.SMEM((LAT,), jnp.int32),
        pltpu.VMEM((LAT, LON), jnp.int32),
        pltpu.VMEM((LAT, OUTW, LON), BF),
        pltpu.VMEM((F, LAT, LON), BF),
        pltpu.VMEM((FP * LAT, LON), F32),
        pltpu.VMEM((LAT, FP, LON), BF),
        pltpu.VMEM((LAT, FP, LON), BF),
        pltpu.VMEM((LAT, FZ, LON), BF),
        pltpu.VMEM((LAT, 2, LON), BF),
        pltpu.VMEM((COLS, 128), BF),
        pltpu.VMEM((LAT, 2 * LON, LON), BF),
        pltpu.VMEM((4, FP, LON), BF),
        pltpu.VMEM((2, FP, 128), BF),
        pltpu.VMEM((4, FP, 128), BF),
        pltpu.VMEM((FP, 128), BF),
        pltpu.VMEM((LAT, LON), F32),
        pltpu.VMEM((NG, SLOTS, COLS), BF),
        pltpu.VMEM((NEXP, ROWS_A, 128), BF),
        pltpu.VMEM((NEXP, ROWS_A, 128), BF),
        pltpu.VMEM((NEXP, ROWS_B, 128), BF),
        pltpu.VMEM((NEXP, ROWS_B, 128), BF),
        pltpu.VMEM((NEXP, ROWS_RET, 128), BF),
        pltpu.VMEM((NEXP, ROWS_RET, 128), BF),
        pltpu.VMEM((W_ROWS, 128), BF),
        pltpu.VMEM((1, F, HID), BF),
        pltpu.VMEM((1, NMID, HID, HID), BF),
        pltpu.VMEM((1, OUTW, HID), BF),
        pltpu.VMEM((SLOTS, FZ), BF),
        pltpu.VMEM((OUTW, SLOTS), BF),
        dma((9,)),
        dma((16,)),
        dma((16,)),
        dma((CHUNKS,)),
        dma((CHUNKS,)),
        dma((CHUNKS,)),
        dma((NEXP,)),
        dma((NEXP,)),
        dma((NEXP,)),
        dma((NEXP,)),
        dma((NEXP,)),
        dma((NEXP,)),
    ]
    adv, tend = pl.pallas_call(
        kernel,
        out_shape=(
            jax.ShapeDtypeStruct((F, LAT, LON), BF),
            jax.ShapeDtypeStruct((LAT, OUTW, LON), BF),
        ),
        in_specs=[anywhere] * 7,
        out_specs=(anywhere, anywhere),
        scratch_shapes=scratch,
        compiler_params=pltpu.CompilerParams(
            collective_id=0, has_side_effects=True, vmem_limit_bytes=60 * 2**20
        ),
        name="step",
    )(
        counts,
        route.reshape(LAT, LON),
        jnp.transpose(state, (2, 0, 1)),
        jnp.transpose(courant, (0, 2, 1)),
        w_in,
        w_mid,
        jnp.transpose(w_out, (0, 2, 1)),
    )
    adv, tend = pl.pallas_call(
        copy_kernel,
        out_shape=(
            jax.ShapeDtypeStruct(adv.shape, BF),
            jax.ShapeDtypeStruct(tend.shape, BF),
        ),
        in_specs=[anywhere] * 2,
        out_specs=(anywhere, anywhere),
        scratch_shapes=[
            pltpu.VMEM(adv.shape, BF),
            pltpu.VMEM(tend.shape, BF),
            dma((8,)),
            dma((8,)),
        ],
        name="hand_over",
    )(adv, tend)
    return jnp.transpose(adv, (1, 2, 0)), jnp.transpose(tend, (0, 2, 1))


def solution(mesh):
    in_specs = (
        P("tile", "grp", None),
        P("tile", "grp", None),
        P("tile", "grp", None, None),
        P("tile"),
        P("tile", None, None),
        P("tile", None, None, None),
        P("tile", None, None),
    )
    out_specs = (P("tile", "grp", None), P("tile", "grp", None))
    return jax.shard_map(
        on_device, mesh=mesh, in_specs=in_specs, out_specs=out_specs, check_vma=False
    )
```

```python
import jax
import jax.numpy as jnp
from jax import lax
from jax.experimental import pallas as pl
from jax.experimental.pallas import tpu as pltpu
from jax.sharding import PartitionSpec as P

BF = jnp.bfloat16
F32 = jnp.float32
MESH = pl.DeviceIdType.MESH

F, HID, OUTW, NMID = 556, 512, 368, 3
FP = 560
FZ = 640
OUTP = 384
LAT, LON, COLS = 16, 128, 2048
CAP = 96
NEXP = 32
NTILE = 32
MAIN = 512
KIN = 576
PARTS = ((0, 256), (256, FP))
ROWS_A = 2 * CAP
ROWS_B = 2 * CAP + CAP // 2
ROWS_RET = 3 * CAP
W_MID = 4 * KIN
W_OUT = W_MID + NMID * 4 * HID
W_ROWS = W_OUT + 4 * OUTP
CHUNKS = 24
CH = W_ROWS // CHUNKS
AHEAD = 3
T_CHUNK, T_HOP, T_RELAY = 12, 52, 175
GB = 4
NG = NEXP // GB
SLOTS = GB * CAP
FIRST = 3


def transposed_dot(a, b):
    return lax.dot_general(a, b, (((1,), (1,)), ((), ())), preferred_element_type=F32)


def kernel(
    counts_hbm, route_hbm, state_hbm, cour_hbm, win_hbm, wmid_hbm, wout_hbm,
    adv_hbm, tend_hbm,
    counts_ref, route_ref, tend_ref,
    st, q32, q0, q1, adv, cour, sel, lon, nsh, xs, xr, hx, place, pall,
    send_a, recv_a, send_b, recv_b, rs, rr, wts, wi, wm, wo, xin, rt,
    lsem, hs_sem, hr_sem, w_s1, w_s2, w_r, fa_s, fa_r, fb_s, fb_r, r_s, r_r,
):
    t = lax.axis_index("tile")
    g = lax.axis_index("grp")
    y, z, x, c = t // 8, t % 8, g // 2, g % 2

    def dest(k):
        j = lax.rem(k * 5, NEXP)
        return lax.rem(y + j // 8, 4), lax.rem(x + (j // 2) % 4, 4), lax.rem(c + j % 2, 2)

    def dest_id(k):
        ty, tx, tc = dest(k)
        return {"tile": ty * 8 + z, "grp": tx * 2 + tc}

    def dest_base(k):
        ty, tx, tc = dest(k)
        return (ty * 8 + tx + 4 * tc) * CAP

    def source_id(k):
        j = lax.rem(k * 5, NEXP)
        ty = lax.rem(y + 4 - j // 8, 4)
        tx = lax.rem(x + 4 - (j // 2) % 4, 4)
        return {"tile": ty * 8 + z, "grp": tx * 2 + lax.rem(c + j % 2, 2)}

    def ring_id(d):
        return {"tile": y * 8 + lax.rem(z + d + 8, 8)}

    def tile_id(d):
        return {"tile": lax.rem(t + d + NTILE, NTILE)}

    def grp_id(d):
        return {"grp": lax.rem(g + d + 8, 8)}

    rel = lax.rem(z + 8 - (x + 4 * c), 8)
    forward_up = (rel >= 1) & (rel <= 3)
    forward_down = rel >= 6
    hop = jnp.where(rel <= 4, rel, 8 - rel)

    barrier = pltpu.get_barrier_semaphore()

    def greet(k, carry):
        pl.semaphore_signal(barrier, inc=1, device_id=dest_id(k), device_id_type=MESH)
        return carry

    lax.fori_loop(1, NEXP, greet, 0)
    for d in (1, -1):
        pl.semaphore_signal(barrier, inc=1, device_id=ring_id(d), device_id_type=MESH)
        pl.semaphore_signal(barrier, inc=1, device_id=tile_id(d), device_id_type=MESH)
        pl.semaphore_signal(barrier, inc=1, device_id=grp_id(d), device_id_type=MESH)

    cp_state = pltpu.make_async_copy(state_hbm, st, lsem.at[0])
    cp_cour = pltpu.make_async_copy(cour_hbm, cour, lsem.at[1])
    cp_wi = pltpu.make_async_copy(win_hbm, wi, lsem.at[2])
    cp_wm = pltpu.make_async_copy(wmid_hbm, wm, lsem.at[3])
    cp_wo = pltpu.make_async_copy(wout_hbm, wo, lsem.at[4])
    cp_adv = pltpu.make_async_copy(st, adv_hbm, lsem.at[5])
    cp_tend = []
    for i in range(0, LAT, 4):
        own = pl.ds(i, 4)
        sem = lsem.at[9 + i // 4]
        cp_tend.append(pltpu.make_async_copy(tend_ref.at[own], tend_hbm.at[own], sem))
    cp_counts = pltpu.make_async_copy(counts_hbm, counts_ref, lsem.at[7])
    cp_route = pltpu.make_async_copy(route_hbm, route_ref, lsem.at[8])
    cp_state.start()
    cp_cour.start()
    cp_counts.start()
    cp_route.start()

    @pl.when(rel == 0)
    def _():
        cp_wi.start()
        cp_wm.start()
        cp_wo.start()

    def halo(n, src, dst, device):
        return pltpu.make_async_remote_copy(
            src, dst, hs_sem.at[n], hr_sem.at[n], device_id=device, device_id_type=MESH
        )

    def halos(step, part, q):
        lo, hi = PARTS[part]
        own = pl.ds(lo, hi - lo)
        b = 8 * step + 4 * part
        return [
            halo(b, q.at[0, own], nsh.at[2 * step, own], tile_id(-1)),
            halo(b + 1, q.at[LAT - 1, own], nsh.at[2 * step + 1, own], tile_id(1)),
            halo(b + 2, xs.at[step, own], xr.at[2 * step + 1, own], grp_id(-1)),
            halo(b + 3, xs.at[step, own], xr.at[2 * step, own], grp_id(1)),
        ]

    halo0 = [halos(0, 0, q0), halos(0, 1, q0)]
    halo1 = [halos(1, 0, q1), halos(1, 1, q1)]

    def wcopy(k, d, sem):
        part = wts.at[pl.ds(pl.multiple_of(k * CH, CH), CH)]
        return pltpu.make_async_remote_copy(
            part, part, sem.at[k], w_r.at[k], device_id=ring_id(d), device_id_type=MESH
        )

    def pass_on(k, carry):
        @pl.when(rel == 0)
        def _():
            wcopy(k, 1, w_s1).start()
            wcopy(k, -1, w_s2).start()

        @pl.when(forward_up)
        def _():
            wcopy(k, 1, w_s1).wait_recv()
            wcopy(k, 1, w_s1).start()

        @pl.when(forward_down)
        def _():
            wcopy(k, -1, w_s1).wait_recv()
            wcopy(k, -1, w_s1).start()

        return carry

    def passed_by(clock):
        behind = clock - T_RELAY - T_HOP * (hop - 1)
        relayed = jnp.where(behind < 0, 0, jnp.minimum(AHEAD + behind // T_CHUNK, CHUNKS))
        begun = jnp.where(clock >= 40, AHEAD, 0)
        begun = jnp.where(clock >= 90, 11, begun)
        begun = jnp.where(clock >= 170, 18, begun)
        begun = jnp.where(clock >= 210, CHUNKS, begun)
        return jnp.where(rel == 0, begun, jnp.where(forward_up | forward_down, relayed, 0))

    def ring(before, now):
        lax.fori_loop(passed_by(before), passed_by(now), pass_on, 0)

    cp_state.wait()

    def widen(i, carry):
        for s in range(4):
            q32[pl.ds(pl.multiple_of((i * 4 + s) * LAT, LAT), LAT), :] = st[i * 4 + s].astype(F32)
        return carry

    lax.fori_loop(0, F // 4, widen, 0)
    q32[F * LAT : FP * LAT, :] = jnp.zeros(((FP - F) * LAT, LON), F32)

    for i in range(LAT):
        q0[i] = q32[pl.ds(i, FP, stride=LAT), :].astype(BF)

    s_row = lax.broadcasted_iota(jnp.int32, (LON, 128), 0)
    s_lane = lax.broadcasted_iota(jnp.int32, (LON, 128), 1)
    for i in range(LAT):
        pick = ((s_row == LON - 1) & (s_lane == i)) | ((s_row == 0) & (s_lane == 64 + i))
        sel[i * LON : (i + 1) * LON, :] = pick.astype(F32).astype(BF)

    def edges(step, part, q):
        lo, hi = PARTS[part]
        row = jnp.concatenate([q[i, lo:hi, :] for i in range(LAT)], axis=1)
        xs[step, lo:hi, :] = jnp.dot(row, sel[...], preferred_element_type=F32).astype(BF)

    edges(0, 0, q0)
    edges(0, 1, q0)

    cp_cour.wait()

    def lon_matrix(i, carry):
        u = cour[i].astype(F32)[0:1]
        pos, neg = jnp.maximum(u, 0.0), jnp.maximum(-u, 0.0)
        top = jnp.where(s_row == s_lane - 1, pos, 0.0)
        top = jnp.where(s_row == s_lane + 1, neg, top)
        top = jnp.where(s_row == s_lane, -(pos + neg), top)
        low = jnp.where((s_row == i) & (s_lane == 0), pos, 0.0)
        low = jnp.where((s_row == 64 + i) & (s_lane == LON - 1), neg, low)
        lon[i, 0:LON, :] = top.astype(BF)
        lon[i, LON : 2 * LON, :] = low.astype(BF)
        return carry

    lax.fori_loop(0, LAT, lon_matrix, 0)

    cp_counts.wait()
    cp_route.wait()

    lat_no = lax.broadcasted_iota(jnp.int32, (LAT, LON), 0)
    lon_no = lax.broadcasted_iota(jnp.int32, (LAT, LON), 1) + g * LON
    reach = jnp.zeros((LAT, LON), jnp.int32)
    for i in range(LAT):
        reach = jnp.where(lat_no == i, counts_ref[i], reach)
    member = jnp.where(lon_no < reach, route_ref[...], -1)
    named = jnp.concatenate([(member == m).astype(F32) for m in range(NEXP)], axis=0).astype(BF)
    before = (
        lax.broadcasted_iota(jnp.int32, (LON, LON), 0)
        < lax.broadcasted_iota(jnp.int32, (LON, LON), 1)
    )
    within = jnp.dot(named, before.astype(F32).astype(BF), preferred_element_type=F32)
    whole = jnp.dot(named, jnp.ones((LON, LON), BF), preferred_element_type=F32).astype(BF)
    r0 = lax.broadcasted_iota(jnp.int32, (NEXP * LAT, NEXP * LAT), 0)
    r1 = lax.broadcasted_iota(jnp.int32, (NEXP * LAT, NEXP * LAT), 1)
    rows_before = ((r0 // LAT == r1 // LAT) & (r1 < r0)).astype(F32).astype(BF)
    number = within + jnp.dot(rows_before, whole, preferred_element_type=F32)
    spot = jnp.full((LAT, LON), -1.0, F32)
    for m in range(NEXP):
        spot = jnp.where(member == m, number[m * LAT : (m + 1) * LAT] + float(m * CAP), spot)
    place[...] = spot

    slot_no = lax.broadcasted_iota(jnp.int32, (CAP, LON), 0)

    def hits(gi, carry):
        for b in range(GB):
            wanted = (slot_no + dest_base(gi * GB + b)).astype(F32)
            for i in range(LAT):
                hit = place[i : i + 1, :] == wanted
                pall[gi, b * CAP : (b + 1) * CAP, i * LON : (i + 1) * LON] = hit.astype(F32).astype(BF)
        return carry

    def lat_step(i, lo, hi, q, south, north, write):
        row = jnp.concatenate([q[i, lo:hi, :], hx[lo:hi, :]], axis=1)
        part = jnp.dot(row, lon[i], preferred_element_type=F32)
        v = cour[i].astype(F32)[1:2]
        half = (hi - lo) // 32 * 16
        for a, b in ((lo, lo + half), (lo + half, hi)):
            mid = q[i, a:b, :].astype(F32)
            lat_up = jnp.where(jnp.broadcast_to(v > 0, (b - a, LON)), south(a, b), north(a, b))
            write(i, a, b, mid + part[a - lo : b - lo] + jnp.abs(v) * (lat_up - mid))

    def advance(q, step, p, write):
        lo, hi = PARTS[p]

        def row(i):
            return lambda a, b: q[i, a:b, :].astype(F32)

        def south_halo(a, b):
            return jnp.where(t == 0, 0.0, nsh[2 * step + 1, a:b, :].astype(F32))

        def north_halo(a, b):
            return jnp.where(t == NTILE - 1, 0.0, nsh[2 * step, a:b, :].astype(F32))

        h = (halo0 if step == 0 else halo1)[p]
        h[2].wait_recv()
        h[3].wait_recv()
        west, east = xr[2 * step, lo:hi].astype(F32), xr[2 * step + 1, lo:hi].astype(F32)
        lane_no = lax.broadcasted_iota(jnp.int32, (hi - lo, 128), 1)
        hx[lo:hi, :] = jnp.where(lane_no < 64, west, east).astype(BF)

        def inner(i, carry):
            lat_step(i, lo, hi, q, row(i - 1), row(i + 1), write)
            return carry

        lax.fori_loop(1, LAT - 1, inner, 0)
        h[0].wait_recv()
        h[1].wait_recv()
        lat_step(0, lo, hi, q, south_halo, row(1), write)
        lat_step(LAT - 1, lo, hi, q, row(LAT - 2), north_halo, write)

    def write_first(i, a, b, new):
        q1[i, a:b, :] = new.astype(BF)

    def write_last(i, a, b, new):
        out = new.astype(BF)
        adv[i, a:b, :] = out
        q32[pl.ds(a * LAT + i, b - a, stride=LAT), :] = out.astype(F32)

    pl.semaphore_wait(barrier, NEXP - 1 + 6)
    for p in range(2):
        for n in (2, 3, 0, 1):
            halo0[p][n].start()

    @pl.when(rel == 0)
    def _():
        cp_wi.wait()
        cp_wm.wait()
        cp_wo.wait()
        for n in range(4):
            wts[n * KIN + 544 : (n + 1) * KIN, :] = jnp.zeros((KIN - 544, 128), BF)
            wts[n * KIN : n * KIN + F, :] = wi[0, :, n * 128 : (n + 1) * 128]
        for k in range(NMID):
            for n in range(4):
                r = W_MID + (k * 4 + n) * HID
                wts[r : r + HID, :] = wm[0, k, :, n * 128 : (n + 1) * 128]
        for n in range(4):
            r = W_OUT + n * OUTP
            wts[r : r + OUTW, :] = wo[0, :, n * 128 : (n + 1) * 128]
            wts[r + OUTW : r + OUTP, :] = jnp.zeros((OUTP - OUTW, 128), BF)

    lax.fori_loop(0, NG, hits, 0)
    for i in range(LAT):
        adv[i, FP:FZ, :] = jnp.zeros((FZ - FP, LON), BF)
        tend_ref[i] = jnp.zeros((OUTW, LON), BF)
    ring(0, 40)
    for p in range(2):
        advance(q0, 0, p, write_first)
        halo1[p][0].start()
        halo1[p][1].start()
        edges(1, p, q1)
        halo1[p][2].start()
        halo1[p][3].start()
        ring((40, 65)[p], (65, 90)[p])

    def forward(p, k):
        src, dst, s_sem, r_sem = ((send_a, recv_a, fa_s, fa_r), (send_b, recv_b, fb_s, fb_r))[p]
        return pltpu.make_async_remote_copy(
            src.at[k], dst.at[k], s_sem.at[k], r_sem.at[k], device_id=dest_id(k), device_id_type=MESH
        )

    def back(k):
        return pltpu.make_async_remote_copy(
            rs.at[k], rr.at[k], r_s.at[k], r_r.at[k], device_id=source_id(k), device_id_type=MESH
        )

    def launch(p, gi, b):
        k = gi * GB + b
        if b > 0:
            forward(p, k).start()
            return

        @pl.when(gi == 0)
        def _():
            if p == 0:
                recv_a[0] = send_a[0]
            else:
                recv_b[0] = send_b[0]

        @pl.when(gi > 0)
        def _():
            forward(p, k).start()

    def pack_a(gi, carry):
        columns = jnp.concatenate([adv[i, 0:256, :] for i in range(LAT)], axis=1)
        rows = transposed_dot(pall[gi], columns)
        for b in range(GB):
            for n in range(2):
                part = rows[b * CAP : (b + 1) * CAP, n * 128 : (n + 1) * 128]
                send_a[gi * GB + b, n * CAP : (n + 1) * CAP, :] = part.astype(BF)
            launch(0, gi, b)
        start = jnp.where(gi < FIRST, 170, 180) + 8 * gi
        ring(start, start + 8)
        return carry

    def pack_b(gi, carry):
        columns = jnp.concatenate([adv[i, 256:FZ, :] for i in range(LAT)], axis=1)
        rows = transposed_dot(pall[gi], columns)
        for b in range(GB):
            for n in range(2):
                part = rows[b * CAP : (b + 1) * CAP, n * 128 : (n + 1) * 128]
                send_b[gi * GB + b, n * CAP : (n + 1) * CAP, :] = part.astype(BF)
            low = rows[b * CAP : b * CAP + CAP // 2, 256:384]
            high = rows[b * CAP + CAP // 2 : (b + 1) * CAP, 256:384]
            send_b[gi * GB + b, 2 * CAP : ROWS_B, :] = (low + pltpu.roll(high, 64, 1)).astype(BF)
            launch(1, gi, b)
        ring(244 + 10 * gi, 254 + 10 * gi)
        return carry

    advance(q1, 1, 0, write_last)
    ring(90, 170)
    lax.fori_loop(0, FIRST, pack_a, 0)
    advance(q1, 1, 1, write_last)
    ring(170 + 8 * FIRST, 180 + 8 * FIRST)
    lax.fori_loop(FIRST, NG, pack_a, 0)
    lax.fori_loop(0, NG, pack_b, 0)

    def narrow(i, carry):
        for s in range(4):
            st[i * 4 + s] = q32[pl.ds(pl.multiple_of((i * 4 + s) * LAT, LAT), LAT), :].astype(BF)
        return carry

    lax.fori_loop(0, F // 4, narrow, 0)
    cp_adv.start()
    ring(244 + 10 * NG, 2000)

    @pl.when((rel == 4) | (rel == 5))
    def _():
        def landed(k, carry):
            wcopy(k, 1, w_s1).wait_recv()
            return carry

        lax.fori_loop(0, CHUNKS, landed, 0)

    def weights(base, rows, parts):
        return jnp.concatenate(
            [wts[base + n * rows : base + (n + 1) * rows, :] for n in range(parts)], axis=1
        )

    def net(gi, carry):
        for b in range(GB):
            k = gi * GB + b
            if b == 0:

                @pl.when(gi > 0)
                def _():
                    forward(0, k).wait_recv()
                    forward(1, k).wait_recv()
            else:
                forward(0, k).wait_recv()
                forward(1, k).wait_recv()
            own = slice(b * CAP, (b + 1) * CAP)
            for n in range(2):
                xin[own, n * 128 : (n + 1) * 128] = recv_a[k, n * CAP : (n + 1) * CAP, :]
                xin[own, 256 + n * 128 : 384 + n * 128] = recv_b[k, n * CAP : (n + 1) * CAP, :]
            both = recv_b[k, 2 * CAP : ROWS_B, :]
            xin[b * CAP : b * CAP + CAP // 2, MAIN:640] = both
            xin[b * CAP + CAP // 2 : (b + 1) * CAP, MAIN:640] = pltpu.roll(
                both.astype(F32), 64, 1
            ).astype(BF)
        h = jnp.dot(xin[:, 0:KIN], weights(0, KIN, 4), preferred_element_type=F32)
        h = jnp.maximum(h, 0.15 * h).astype(BF)
        for layer in range(NMID):
            w = weights(W_MID + layer * 4 * HID, HID, 4)
            h = jnp.dot(h, w, preferred_element_type=F32)
            h = jnp.maximum(h, 0.15 * h).astype(BF)
        out = transposed_dot(h, weights(W_OUT, OUTP, 4)).astype(BF)
        for b in range(GB):
            k = gi * GB + b
            for n in range(3):
                rs[k, n * CAP : (n + 1) * CAP, :] = out[
                    b * CAP : (b + 1) * CAP, n * 128 : (n + 1) * 128
                ]
            if b == 0:

                @pl.when(gi == 0)
                def _():
                    rr[0] = rs[0]

                @pl.when(gi > 0)
                def _():
                    back(k).start()
            else:
                back(k).start()
        return carry

    lax.fori_loop(0, NG, net, 0)

    for hs in halo0 + halo1:
        for h in hs:
            h.wait_send()

    def sent(k, carry):
        forward(0, k).wait_send()
        forward(1, k).wait_send()
        return carry

    lax.fori_loop(1, NEXP, sent, 0)

    def passed_on(k, carry):
        wcopy(k, 1, w_s1).wait_send()
        return carry

    @pl.when((rel != 4) & (rel != 5))
    def _():
        lax.fori_loop(0, CHUNKS, passed_on, 0)

    @pl.when(rel == 0)
    def _():
        def passed_down(k, carry):
            wcopy(k, -1, w_s2).wait_send()
            return carry

        lax.fori_loop(0, CHUNKS, passed_down, 0)

    cp_adv.wait()

    def unpack(gi, carry):
        for b in range(GB):
            k = gi * GB + b
            if b == 0:

                @pl.when(gi > 0)
                def _():
                    back(k).wait_recv()
            else:
                back(k).wait_recv()
        block = jnp.concatenate(
            [
                jnp.concatenate(
                    [rr[gi * GB + b, n * CAP : (n + 1) * CAP, :] for n in range(3)], axis=1
                )
                for b in range(GB)
            ],
            axis=0,
        )
        rt[...] = jnp.transpose(block.astype(F32)).astype(BF)[0:OUTW]
        for i in range(0, LAT, 4):
            got = jnp.dot(
                rt[...], pall[gi, :, i * LON : (i + 4) * LON], preferred_element_type=F32
            )
            for s in range(4):
                old = tend_ref[i + s].astype(F32)
                tend_ref[i + s] = (old + got[:, s * LON : (s + 1) * LON]).astype(BF)

            @pl.when(gi == NG - 1)
            def _():
                cp_tend[i // 4].start()

        for b in range(GB):
            k = gi * GB + b
            if b == 0:

                @pl.when(gi > 0)
                def _():
                    back(k).wait_send()
            else:
                back(k).wait_send()
        return carry

    lax.fori_loop(0, NG, unpack, 0)

    for one in cp_tend:
        one.wait()


def copy_kernel(adv_in, tend_in, adv_out, tend_out, adv_v, tend_v, sem_in, sem_out):
    into, out = [], []
    for j, (a, v, b, n) in enumerate(
        ((adv_in, adv_v, adv_out, F // 4), (tend_in, tend_v, tend_out, LAT // 4))
    ):
        for i in range(4):
            part = pl.ds(i * n, n)
            into.append(pltpu.make_async_copy(a.at[part], v.at[part], sem_in.at[4 * j + i]))
            out.append(pltpu.make_async_copy(v.at[part], b.at[part], sem_out.at[4 * j + i]))
    for one in into:
        one.start()
    for one, two in zip(into, out):
        one.wait()
        two.start()
    for two in out:
        two.wait()


def on_device(state, courant, route, counts, w_in, w_mid, w_out):
    anywhere = pl.BlockSpec(memory_space=pl.ANY)
    dma = pltpu.SemaphoreType.DMA
    scratch = [
        pltpu.SMEM((LAT,), jnp.int32),
        pltpu.VMEM((LAT, LON), jnp.int32),
        pltpu.VMEM((LAT, OUTW, LON), BF),
        pltpu.VMEM((F, LAT, LON), BF),
        pltpu.VMEM((FP * LAT, LON), F32),
        pltpu.VMEM((LAT, FP, LON), BF),
        pltpu.VMEM((LAT, FP, LON), BF),
        pltpu.VMEM((LAT, FZ, LON), BF),
        pltpu.VMEM((LAT, 2, LON), BF),
        pltpu.VMEM((COLS, 128), BF),
        pltpu.VMEM((LAT, 2 * LON, LON), BF),
        pltpu.VMEM((4, FP, LON), BF),
        pltpu.VMEM((2, FP, 128), BF),
        pltpu.VMEM((4, FP, 128), BF),
        pltpu.VMEM((FP, 128), BF),
        pltpu.VMEM((LAT, LON), F32),
        pltpu.VMEM((NG, SLOTS, COLS), BF),
        pltpu.VMEM((NEXP, ROWS_A, 128), BF),
        pltpu.VMEM((NEXP, ROWS_A, 128), BF),
        pltpu.VMEM((NEXP, ROWS_B, 128), BF),
        pltpu.VMEM((NEXP, ROWS_B, 128), BF),
        pltpu.VMEM((NEXP, ROWS_RET, 128), BF),
        pltpu.VMEM((NEXP, ROWS_RET, 128), BF),
        pltpu.VMEM((W_ROWS, 128), BF),
        pltpu.VMEM((1, F, HID), BF),
        pltpu.VMEM((1, NMID, HID, HID), BF),
        pltpu.VMEM((1, OUTW, HID), BF),
        pltpu.VMEM((SLOTS, FZ), BF),
        pltpu.VMEM((OUTW, SLOTS), BF),
        dma((13,)),
        dma((16,)),
        dma((16,)),
        dma((CHUNKS,)),
        dma((CHUNKS,)),
        dma((CHUNKS,)),
        dma((NEXP,)),
        dma((NEXP,)),
        dma((NEXP,)),
        dma((NEXP,)),
        dma((NEXP,)),
        dma((NEXP,)),
    ]
    adv, tend = pl.pallas_call(
        kernel,
        out_shape=(
            jax.ShapeDtypeStruct((F, LAT, LON), BF),
            jax.ShapeDtypeStruct((LAT, OUTW, LON), BF),
        ),
        in_specs=[anywhere] * 7,
        out_specs=(anywhere, anywhere),
        scratch_shapes=scratch,
        compiler_params=pltpu.CompilerParams(
            collective_id=0, has_side_effects=True, vmem_limit_bytes=60 * 2**20
        ),
        name="step",
    )(
        counts,
        route.reshape(LAT, LON),
        jnp.transpose(state, (2, 0, 1)),
        jnp.transpose(courant, (0, 2, 1)),
        w_in,
        w_mid,
        jnp.transpose(w_out, (0, 2, 1)),
    )
    adv, tend = pl.pallas_call(
        copy_kernel,
        out_shape=(
            jax.ShapeDtypeStruct(adv.shape, BF),
            jax.ShapeDtypeStruct(tend.shape, BF),
        ),
        in_specs=[anywhere] * 2,
        out_specs=(anywhere, anywhere),
        scratch_shapes=[
            pltpu.VMEM(adv.shape, BF),
            pltpu.VMEM(tend.shape, BF),
            dma((8,)),
            dma((8,)),
        ],
        name="hand_over",
    )(adv, tend)
    return jnp.transpose(adv, (1, 2, 0)), jnp.transpose(tend, (0, 2, 1))


def solution(mesh):
    in_specs = (
        P("tile", "grp", None),
        P("tile", "grp", None),
        P("tile", "grp", None, None),
        P("tile"),
        P("tile", None, None),
        P("tile", None, None, None),
        P("tile", None, None),
    )
    out_specs = (P("tile", "grp", None), P("tile", "grp", None))
    return jax.shard_map(
        on_device, mesh=mesh, in_specs=in_specs, out_specs=out_specs, check_vma=False
    )
```

```python
import jax
import jax.numpy as jnp
from jax import lax
from jax.experimental import pallas as pl
from jax.experimental.pallas import tpu as pltpu
from jax.sharding import PartitionSpec as P

BF = jnp.bfloat16
F32 = jnp.float32
MESH = pl.DeviceIdType.MESH

F, HID, OUTW, NMID = 556, 512, 368, 3
FP = 560
FZ = 640
OUTP = 384
LAT, LON, COLS = 16, 128, 2048
CAP = 96
NEXP = 32
NTILE = 32
MAIN = 512
KIN = 576
PARTS = ((0, 256), (256, FP))
ROWS_A = 2 * CAP
ROWS_B = 2 * CAP + CAP // 2
ROWS_RET = 3 * CAP
W_MID = 4 * KIN
W_OUT = W_MID + NMID * 4 * HID
W_ROWS = W_OUT + 4 * OUTP
CHUNKS = 24
CH = W_ROWS // CHUNKS
AHEAD = 3
T_CHUNK, T_HOP, T_RELAY = 12, 52, 175
GB = 4
NG = NEXP // GB
SLOTS = GB * CAP
FIRST = 3


def transposed_dot(a, b):
    return lax.dot_general(a, b, (((1,), (1,)), ((), ())), preferred_element_type=F32)


def kernel(
    counts_hbm, route_hbm, state_hbm, cour_hbm, win_hbm, wmid_hbm, wout_hbm,
    adv_hbm, tend_hbm,
    counts_ref, route_ref, tend_ref,
    st, q32, q0, q1, adv, cour, sel, lon, nsh, xs, xr, hx, place, pall,
    send_a, recv_a, send_b, recv_b, rs, rr, wts, wi, wm, wo, xin, rt,
    lsem, hs_sem, hr_sem, w_s1, w_s2, w_r, fa_s, fa_r, fb_s, fb_r, r_s, r_r,
):
    t = lax.axis_index("tile")
    g = lax.axis_index("grp")
    y, z, x, c = t // 8, t % 8, g // 2, g % 2

    def dest(k):
        j = lax.rem(k * 5, NEXP)
        return lax.rem(y + j // 8, 4), lax.rem(x + (j // 2) % 4, 4), lax.rem(c + j % 2, 2)

    def dest_id(k):
        ty, tx, tc = dest(k)
        return {"tile": ty * 8 + z, "grp": tx * 2 + tc}

    def dest_base(k):
        ty, tx, tc = dest(k)
        return (ty * 8 + tx + 4 * tc) * CAP

    def source_id(k):
        j = lax.rem(k * 5, NEXP)
        ty = lax.rem(y + 4 - j // 8, 4)
        tx = lax.rem(x + 4 - (j // 2) % 4, 4)
        return {"tile": ty * 8 + z, "grp": tx * 2 + lax.rem(c + j % 2, 2)}

    def ring_id(d):
        return {"tile": y * 8 + lax.rem(z + d + 8, 8)}

    def tile_id(d):
        return {"tile": lax.rem(t + d + NTILE, NTILE)}

    def grp_id(d):
        return {"grp": lax.rem(g + d + 8, 8)}

    rel = lax.rem(z + 8 - (x + 4 * c), 8)
    forward_up = (rel >= 1) & (rel <= 3)
    forward_down = rel >= 6
    hop = jnp.where(rel <= 4, rel, 8 - rel)

    barrier = pltpu.get_barrier_semaphore()

    def greet(k, carry):
        pl.semaphore_signal(barrier, inc=1, device_id=dest_id(k), device_id_type=MESH)
        return carry

    lax.fori_loop(1, NEXP, greet, 0)
    for d in (1, -1):
        pl.semaphore_signal(barrier, inc=1, device_id=ring_id(d), device_id_type=MESH)
        pl.semaphore_signal(barrier, inc=1, device_id=tile_id(d), device_id_type=MESH)
        pl.semaphore_signal(barrier, inc=1, device_id=grp_id(d), device_id_type=MESH)

    cp_state = pltpu.make_async_copy(state_hbm, st, lsem.at[0])
    cp_cour = pltpu.make_async_copy(cour_hbm, cour, lsem.at[1])
    cp_wi = pltpu.make_async_copy(win_hbm, wi, lsem.at[2])
    cp_wm = pltpu.make_async_copy(wmid_hbm, wm, lsem.at[3])
    cp_wo = pltpu.make_async_copy(wout_hbm, wo, lsem.at[4])
    cp_adv = pltpu.make_async_copy(st, adv_hbm, lsem.at[5])
    cp_tend = []
    for i in range(0, LAT, 4):
        own = pl.ds(i, 4)
        sem = lsem.at[9 + i // 4]
        cp_tend.append(pltpu.make_async_copy(tend_ref.at[own], tend_hbm.at[own], sem))
    cp_counts = pltpu.make_async_copy(counts_hbm, counts_ref, lsem.at[7])
    cp_route = pltpu.make_async_copy(route_hbm, route_ref, lsem.at[8])
    cp_state.start()
    cp_cour.start()
    cp_counts.start()
    cp_route.start()

    @pl.when(rel == 0)
    def _():
        cp_wi.start()
        cp_wm.start()
        cp_wo.start()

    def halo(n, src, dst, device):
        return pltpu.make_async_remote_copy(
            src, dst, hs_sem.at[n], hr_sem.at[n], device_id=device, device_id_type=MESH
        )

    def halos(step, part, q):
        lo, hi = PARTS[part]
        own = pl.ds(lo, hi - lo)
        b = 8 * step + 4 * part
        return [
            halo(b, q.at[0, own], nsh.at[2 * step, own], tile_id(-1)),
            halo(b + 1, q.at[LAT - 1, own], nsh.at[2 * step + 1, own], tile_id(1)),
            halo(b + 2, xs.at[step, own], xr.at[2 * step + 1, own], grp_id(-1)),
            halo(b + 3, xs.at[step, own], xr.at[2 * step, own], grp_id(1)),
        ]

    halo0 = [halos(0, 0, q0), halos(0, 1, q0)]
    halo1 = [halos(1, 0, q1), halos(1, 1, q1)]

    def wcopy(k, d, sem):
        part = wts.at[pl.ds(pl.multiple_of(k * CH, CH), CH)]
        return pltpu.make_async_remote_copy(
            part, part, sem.at[k], w_r.at[k], device_id=ring_id(d), device_id_type=MESH
        )

    def pass_on(k, carry):
        @pl.when(rel == 0)
        def _():
            wcopy(k, 1, w_s1).start()
            wcopy(k, -1, w_s2).start()

        @pl.when(forward_up)
        def _():
            wcopy(k, 1, w_s1).wait_recv()
            wcopy(k, 1, w_s1).start()

        @pl.when(forward_down)
        def _():
            wcopy(k, -1, w_s1).wait_recv()
            wcopy(k, -1, w_s1).start()

        return carry

    def passed_by(clock):
        behind = clock - T_RELAY - T_HOP * (hop - 1)
        relayed = jnp.where(behind < 0, 0, jnp.minimum(AHEAD + behind // T_CHUNK, CHUNKS))
        begun = jnp.where(clock >= 40, AHEAD, 0)
        begun = jnp.where(clock >= 90, 11, begun)
        begun = jnp.where(clock >= 170, 18, begun)
        begun = jnp.where(clock >= 210, CHUNKS, begun)
        return jnp.where(rel == 0, begun, jnp.where(forward_up | forward_down, relayed, 0))

    def ring(before, now):
        lax.fori_loop(passed_by(before), passed_by(now), pass_on, 0)

    cp_state.wait()

    def widen(i, carry):
        for s in range(4):
            q32[pl.ds(pl.multiple_of((i * 4 + s) * LAT, LAT), LAT), :] = st[i * 4 + s].astype(F32)
        return carry

    lax.fori_loop(0, F // 4, widen, 0)
    q32[F * LAT : FP * LAT, :] = jnp.zeros(((FP - F) * LAT, LON), F32)

    for i in range(LAT):
        q0[i] = q32[pl.ds(i, FP, stride=LAT), :].astype(BF)

    s_row = lax.broadcasted_iota(jnp.int32, (LON, 128), 0)
    s_lane = lax.broadcasted_iota(jnp.int32, (LON, 128), 1)
    for i in range(LAT):
        pick = ((s_row == LON - 1) & (s_lane == i)) | ((s_row == 0) & (s_lane == 64 + i))
        sel[i * LON : (i + 1) * LON, :] = pick.astype(F32).astype(BF)

    def edges(step, part, q):
        lo, hi = PARTS[part]
        row = jnp.concatenate([q[i, lo:hi, :] for i in range(LAT)], axis=1)
        xs[step, lo:hi, :] = jnp.dot(row, sel[...], preferred_element_type=F32).astype(BF)

    edges(0, 0, q0)
    edges(0, 1, q0)

    cp_cour.wait()

    def lon_matrix(i, carry):
        u = cour[i].astype(F32)[0:1]
        pos, neg = jnp.maximum(u, 0.0), jnp.maximum(-u, 0.0)
        top = jnp.where(s_row == s_lane - 1, pos, 0.0)
        top = jnp.where(s_row == s_lane + 1, neg, top)
        top = jnp.where(s_row == s_lane, -(pos + neg), top)
        low = jnp.where((s_row == i) & (s_lane == 0), pos, 0.0)
        low = jnp.where((s_row == 64 + i) & (s_lane == LON - 1), neg, low)
        lon[i, 0:LON, :] = top.astype(BF)
        lon[i, LON : 2 * LON, :] = low.astype(BF)
        return carry

    lax.fori_loop(0, LAT, lon_matrix, 0)

    cp_counts.wait()
    cp_route.wait()

    lat_no = lax.broadcasted_iota(jnp.int32, (LAT, LON), 0)
    lon_no = lax.broadcasted_iota(jnp.int32, (LAT, LON), 1) + g * LON
    reach = jnp.zeros((LAT, LON), jnp.int32)
    for i in range(LAT):
        reach = jnp.where(lat_no == i, counts_ref[i], reach)
    member = jnp.where(lon_no < reach, route_ref[...], -1)
    named = jnp.concatenate([(member == m).astype(F32) for m in range(NEXP)], axis=0).astype(BF)
    before = (
        lax.broadcasted_iota(jnp.int32, (LON, LON), 0)
        < lax.broadcasted_iota(jnp.int32, (LON, LON), 1)
    )
    within = jnp.dot(named, before.astype(F32).astype(BF), preferred_element_type=F32)
    whole = jnp.dot(named, jnp.ones((LON, LON), BF), preferred_element_type=F32).astype(BF)
    r0 = lax.broadcasted_iota(jnp.int32, (NEXP * LAT, NEXP * LAT), 0)
    r1 = lax.broadcasted_iota(jnp.int32, (NEXP * LAT, NEXP * LAT), 1)
    rows_before = ((r0 // LAT == r1 // LAT) & (r1 < r0)).astype(F32).astype(BF)
    number = within + jnp.dot(rows_before, whole, preferred_element_type=F32)
    spot = jnp.full((LAT, LON), -1.0, F32)
    for m in range(NEXP):
        spot = jnp.where(member == m, number[m * LAT : (m + 1) * LAT] + float(m * CAP), spot)
    place[...] = spot

    slot_no = lax.broadcasted_iota(jnp.int32, (CAP, LON), 0)

    def hits(gi, carry):
        for b in range(GB):
            wanted = (slot_no + dest_base(gi * GB + b)).astype(F32)
            for i in range(LAT):
                hit = place[i : i + 1, :] == wanted
                pall[gi, b * CAP : (b + 1) * CAP, i * LON : (i + 1) * LON] = hit.astype(F32).astype(BF)
        return carry

    def lat_step(i, lo, hi, q, south, north, write):
        row = jnp.concatenate([q[i, lo:hi, :], hx[lo:hi, :]], axis=1)
        part = jnp.dot(row, lon[i], preferred_element_type=F32)
        v = cour[i].astype(F32)[1:2]
        half = (hi - lo) // 32 * 16
        for a, b in ((lo, lo + half), (lo + half, hi)):
            mid = q[i, a:b, :].astype(F32)
            lat_up = jnp.where(jnp.broadcast_to(v > 0, (b - a, LON)), south(a, b), north(a, b))
            write(i, a, b, mid + part[a - lo : b - lo] + jnp.abs(v) * (lat_up - mid))

    def advance(q, step, p, write):
        lo, hi = PARTS[p]

        def row(i):
            return lambda a, b: q[i, a:b, :].astype(F32)

        def south_halo(a, b):
            return jnp.where(t == 0, 0.0, nsh[2 * step + 1, a:b, :].astype(F32))

        def north_halo(a, b):
            return jnp.where(t == NTILE - 1, 0.0, nsh[2 * step, a:b, :].astype(F32))

        h = (halo0 if step == 0 else halo1)[p]
        h[2].wait_recv()
        h[3].wait_recv()
        west, east = xr[2 * step, lo:hi].astype(F32), xr[2 * step + 1, lo:hi].astype(F32)
        lane_no = lax.broadcasted_iota(jnp.int32, (hi - lo, 128), 1)
        hx[lo:hi, :] = jnp.where(lane_no < 64, west, east).astype(BF)

        def inner(i, carry):
            lat_step(i, lo, hi, q, row(i - 1), row(i + 1), write)
            return carry

        lax.fori_loop(1, LAT - 1, inner, 0)
        h[0].wait_recv()
        h[1].wait_recv()
        lat_step(0, lo, hi, q, south_halo, row(1), write)
        lat_step(LAT - 1, lo, hi, q, row(LAT - 2), north_halo, write)

    def write_first(i, a, b, new):
        q1[i, a:b, :] = new.astype(BF)

    def write_last(i, a, b, new):
        out = new.astype(BF)
        adv[i, a:b, :] = out
        q32[pl.ds(a * LAT + i, b - a, stride=LAT), :] = out.astype(F32)

    pl.semaphore_wait(barrier, NEXP - 1 + 6)
    for p in range(2):
        for n in (2, 3, 0, 1):
            halo0[p][n].start()

    @pl.when(rel == 0)
    def _():
        cp_wi.wait()
        cp_wm.wait()
        cp_wo.wait()
        for n in range(4):
            wts[n * KIN + 544 : (n + 1) * KIN, :] = jnp.zeros((KIN - 544, 128), BF)
            wts[n * KIN : n * KIN + F, :] = wi[0, :, n * 128 : (n + 1) * 128]
        for k in range(NMID):
            for n in range(4):
                r = W_MID + (k * 4 + n) * HID
                wts[r : r + HID, :] = wm[0, k, :, n * 128 : (n + 1) * 128]
        for n in range(4):
            r = W_OUT + n * OUTP
            wts[r : r + OUTW, :] = wo[0, :, n * 128 : (n + 1) * 128]
            wts[r + OUTW : r + OUTP, :] = jnp.zeros((OUTP - OUTW, 128), BF)

    lax.fori_loop(0, NG, hits, 0)
    for i in range(LAT):
        adv[i, FP:FZ, :] = jnp.zeros((FZ - FP, LON), BF)
        tend_ref[i] = jnp.zeros((OUTW, LON), BF)
    ring(0, 40)
    for p in range(2):
        advance(q0, 0, p, write_first)
        halo1[p][0].start()
        halo1[p][1].start()
        edges(1, p, q1)
        halo1[p][2].start()
        halo1[p][3].start()
        ring((40, 65)[p], (65, 90)[p])

    def forward(p, k):
        src, dst, s_sem, r_sem = ((send_a, recv_a, fa_s, fa_r), (send_b, recv_b, fb_s, fb_r))[p]
        return pltpu.make_async_remote_copy(
            src.at[k], dst.at[k], s_sem.at[k], r_sem.at[k], device_id=dest_id(k), device_id_type=MESH
        )

    def back(k):
        return pltpu.make_async_remote_copy(
            rs.at[k], rr.at[k], r_s.at[k], r_r.at[k], device_id=source_id(k), device_id_type=MESH
        )

    def launch(p, gi, b):
        k = gi * GB + b
        if b > 0:
            forward(p, k).start()
            return

        @pl.when(gi == 0)
        def _():
            if p == 0:
                recv_a[0] = send_a[0]
            else:
                recv_b[0] = send_b[0]

        @pl.when(gi > 0)
        def _():
            forward(p, k).start()

    def pack_a(gi, carry):
        columns = jnp.concatenate([adv[i, 0:256, :] for i in range(LAT)], axis=1)
        rows = transposed_dot(pall[gi], columns)
        for b in range(GB):
            for n in range(2):
                part = rows[b * CAP : (b + 1) * CAP, n * 128 : (n + 1) * 128]
                send_a[gi * GB + b, n * CAP : (n + 1) * CAP, :] = part.astype(BF)
            launch(0, gi, b)
        start = jnp.where(gi < FIRST, 170, 180) + 8 * gi
        ring(start, start + 8)
        return carry

    def pack_b(gi, carry):
        columns = jnp.concatenate([adv[i, 256:FZ, :] for i in range(LAT)], axis=1)
        rows = transposed_dot(pall[gi], columns)
        for b in range(GB):
            for n in range(2):
                part = rows[b * CAP : (b + 1) * CAP, n * 128 : (n + 1) * 128]
                send_b[gi * GB + b, n * CAP : (n + 1) * CAP, :] = part.astype(BF)
            low = rows[b * CAP : b * CAP + CAP // 2, 256:384]
            high = rows[b * CAP + CAP // 2 : (b + 1) * CAP, 256:384]
            send_b[gi * GB + b, 2 * CAP : ROWS_B, :] = (low + pltpu.roll(high, 64, 1)).astype(BF)
            launch(1, gi, b)
        ring(244 + 10 * gi, 254 + 10 * gi)
        return carry

    advance(q1, 1, 0, write_last)
    ring(90, 170)
    lax.fori_loop(0, FIRST, pack_a, 0)
    advance(q1, 1, 1, write_last)
    ring(170 + 8 * FIRST, 180 + 8 * FIRST)
    lax.fori_loop(FIRST, NG, pack_a, 0)
    lax.fori_loop(0, NG, pack_b, 0)

    def narrow(i, carry):
        for s in range(4):
            st[i * 4 + s] = q32[pl.ds(pl.multiple_of((i * 4 + s) * LAT, LAT), LAT), :].astype(BF)
        return carry

    lax.fori_loop(0, F // 4, narrow, 0)
    cp_adv.start()
    ring(244 + 10 * NG, 2000)

    @pl.when((rel == 4) | (rel == 5))
    def _():
        def landed(k, carry):
            wcopy(k, 1, w_s1).wait_recv()
            return carry

        lax.fori_loop(0, CHUNKS, landed, 0)

    def weights(base, rows, parts):
        return jnp.concatenate(
            [wts[base + n * rows : base + (n + 1) * rows, :] for n in range(parts)], axis=1
        )

    def net(gi, carry):
        for b in range(GB):
            k = gi * GB + b
            if b == 0:

                @pl.when(gi > 0)
                def _():
                    forward(0, k).wait_recv()
                    forward(1, k).wait_recv()
            else:
                forward(0, k).wait_recv()
                forward(1, k).wait_recv()
            own = slice(b * CAP, (b + 1) * CAP)
            for n in range(2):
                xin[own, n * 128 : (n + 1) * 128] = recv_a[k, n * CAP : (n + 1) * CAP, :]
                xin[own, 256 + n * 128 : 384 + n * 128] = recv_b[k, n * CAP : (n + 1) * CAP, :]
            both = recv_b[k, 2 * CAP : ROWS_B, :]
            xin[b * CAP : b * CAP + CAP // 2, MAIN:640] = both
            xin[b * CAP + CAP // 2 : (b + 1) * CAP, MAIN:640] = pltpu.roll(
                both.astype(F32), 64, 1
            ).astype(BF)
        h = jnp.dot(xin[:, 0:KIN], weights(0, KIN, 4), preferred_element_type=F32)
        h = jnp.maximum(h, 0.15 * h).astype(BF)
        for layer in range(NMID):
            w = weights(W_MID + layer * 4 * HID, HID, 4)
            h = jnp.dot(h, w, preferred_element_type=F32)
            h = jnp.maximum(h, 0.15 * h).astype(BF)
        out = transposed_dot(h, weights(W_OUT, OUTP, 4)).astype(BF)
        for b in range(GB):
            k = gi * GB + b
            for n in range(3):
                rs[k, n * CAP : (n + 1) * CAP, :] = out[
                    b * CAP : (b + 1) * CAP, n * 128 : (n + 1) * 128
                ]
            if b == 0:

                @pl.when(gi == 0)
                def _():
                    rr[0] = rs[0]

                @pl.when(gi > 0)
                def _():
                    back(k).start()
            else:
                back(k).start()
        return carry

    lax.fori_loop(0, NG, net, 0)

    for hs in halo0 + halo1:
        for h in hs:
            h.wait_send()

    def sent(k, carry):
        forward(0, k).wait_send()
        forward(1, k).wait_send()
        return carry

    lax.fori_loop(1, NEXP, sent, 0)

    def passed_on(k, carry):
        wcopy(k, 1, w_s1).wait_send()
        return carry

    @pl.when((rel != 4) & (rel != 5))
    def _():
        lax.fori_loop(0, CHUNKS, passed_on, 0)

    @pl.when(rel == 0)
    def _():
        def passed_down(k, carry):
            wcopy(k, -1, w_s2).wait_send()
            return carry

        lax.fori_loop(0, CHUNKS, passed_down, 0)

    cp_adv.wait()

    def unpack(gi, carry):
        for b in range(GB):
            k = gi * GB + b
            if b == 0:

                @pl.when(gi > 0)
                def _():
                    back(k).wait_recv()
            else:
                back(k).wait_recv()
        block = jnp.concatenate(
            [
                jnp.concatenate(
                    [rr[gi * GB + b, n * CAP : (n + 1) * CAP, :] for n in range(3)], axis=1
                )
                for b in range(GB)
            ],
            axis=0,
        )
        rt[...] = jnp.transpose(block.astype(F32)).astype(BF)[0:OUTW]
        for i in range(0, LAT, 4):
            got = jnp.dot(
                rt[...], pall[gi, :, i * LON : (i + 4) * LON], preferred_element_type=F32
            )
            for s in range(4):
                old = tend_ref[i + s].astype(F32)
                tend_ref[i + s] = (old + got[:, s * LON : (s + 1) * LON]).astype(BF)

            @pl.when(gi == NG - 1)
            def _():
                cp_tend[i // 4].start()

        for b in range(GB):
            k = gi * GB + b
            if b == 0:

                @pl.when(gi > 0)
                def _():
                    back(k).wait_send()
            else:
                back(k).wait_send()
        return carry

    lax.fori_loop(0, NG, unpack, 0)

    for one in cp_tend:
        one.wait()


def copy_kernel(adv_in, tend_in, adv_out, tend_out, adv_v, tend_v, sem_in, sem_out):
    into, out = [], []
    for j, (a, v, b, n) in enumerate(
        ((adv_in, adv_v, adv_out, F // 4), (tend_in, tend_v, tend_out, LAT // 4))
    ):
        for i in range(4):
            part = pl.ds(i * n, n)
            into.append(pltpu.make_async_copy(a.at[part], v.at[part], sem_in.at[4 * j + i]))
            out.append(pltpu.make_async_copy(v.at[part], b.at[part], sem_out.at[4 * j + i]))
    for one in into:
        one.start()
    for one, two in zip(into, out):
        one.wait()
        two.start()
    for two in out:
        two.wait()


def on_device(state, courant, route, counts, w_in, w_mid, w_out):
    anywhere = pl.BlockSpec(memory_space=pl.ANY)
    dma = pltpu.SemaphoreType.DMA
    scratch = [
        pltpu.SMEM((LAT,), jnp.int32),
        pltpu.VMEM((LAT, LON), jnp.int32),
        pltpu.VMEM((LAT, OUTW, LON), BF),
        pltpu.VMEM((F, LAT, LON), BF),
        pltpu.VMEM(((FP + 1) * LAT, LON), F32),
        pltpu.VMEM((LAT, FP, LON), BF),
        pltpu.VMEM((LAT, FP, LON), BF),
        pltpu.VMEM((LAT, FZ, LON), BF),
        pltpu.VMEM((LAT, 2, LON), BF),
        pltpu.VMEM((COLS, 128), BF),
        pltpu.VMEM((LAT, 2 * LON, LON), BF),
        pltpu.VMEM((4, FP, LON), BF),
        pltpu.VMEM((2, FP, 128), BF),
        pltpu.VMEM((4, FP, 128), BF),
        pltpu.VMEM((FP, 128), BF),
        pltpu.VMEM((LAT, LON), F32),
        pltpu.VMEM((NG, SLOTS, COLS), BF),
        pltpu.VMEM((NEXP, ROWS_A, 128), BF),
        pltpu.VMEM((NEXP, ROWS_A, 128), BF),
        pltpu.VMEM((NEXP, ROWS_B, 128), BF),
        pltpu.VMEM((NEXP, ROWS_B, 128), BF),
        pltpu.VMEM((NEXP, ROWS_RET, 128), BF),
        pltpu.VMEM((NEXP, ROWS_RET, 128), BF),
        pltpu.VMEM((W_ROWS, 128), BF),
        pltpu.VMEM((1, F, HID), BF),
        pltpu.VMEM((1, NMID, HID, HID), BF),
        pltpu.VMEM((1, OUTW, HID), BF),
        pltpu.VMEM((SLOTS, FZ), BF),
        pltpu.VMEM((OUTW, SLOTS), BF),
        dma((13,)),
        dma((16,)),
        dma((16,)),
        dma((CHUNKS,)),
        dma((CHUNKS,)),
        dma((CHUNKS,)),
        dma((NEXP,)),
        dma((NEXP,)),
        dma((NEXP,)),
        dma((NEXP,)),
        dma((NEXP,)),
        dma((NEXP,)),
    ]
    adv, tend = pl.pallas_call(
        kernel,
        out_shape=(
            jax.ShapeDtypeStruct((F, LAT, LON), BF),
            jax.ShapeDtypeStruct((LAT, OUTW, LON), BF),
        ),
        in_specs=[anywhere] * 7,
        out_specs=(anywhere, anywhere),
        scratch_shapes=scratch,
        compiler_params=pltpu.CompilerParams(
            collective_id=0, has_side_effects=True, vmem_limit_bytes=60 * 2**20
        ),
        name="step",
    )(
        counts,
        route.reshape(LAT, LON),
        jnp.transpose(state, (2, 0, 1)),
        jnp.transpose(courant, (0, 2, 1)),
        w_in,
        w_mid,
        jnp.transpose(w_out, (0, 2, 1)),
    )
    adv, tend = pl.pallas_call(
        copy_kernel,
        out_shape=(
            jax.ShapeDtypeStruct(adv.shape, BF),
            jax.ShapeDtypeStruct(tend.shape, BF),
        ),
        in_specs=[anywhere] * 2,
        out_specs=(anywhere, anywhere),
        scratch_shapes=[
            pltpu.VMEM(adv.shape, BF),
            pltpu.VMEM(tend.shape, BF),
            dma((8,)),
            dma((8,)),
        ],
        name="hand_over",
    )(adv, tend)
    return jnp.transpose(adv, (1, 2, 0)), jnp.transpose(tend, (0, 2, 1))


def solution(mesh):
    in_specs = (
        P("tile", "grp", None),
        P("tile", "grp", None),
        P("tile", "grp", None, None),
        P("tile"),
        P("tile", None, None),
        P("tile", None, None, None),
        P("tile", None, None),
    )
    out_specs = (P("tile", "grp", None), P("tile", "grp", None))
    return jax.shard_map(
        on_device, mesh=mesh, in_specs=in_specs, out_specs=out_specs, check_vma=False
    )
```
